32 devices in a mesh: cell: 32 (over z, y, x, core).
Axes of the slice: x: 2, y: 2, z: 4, core: 2. Of those that a mesh axis runs over, the one named last changes fastest.
Arguments:
- features: bfloat16 [8192, 512], P('cell'), may hold values from -6 to 6
- radial: bfloat16 [8192, 8, 128], P('cell'), may hold values from 0 to 1
- neighbours: int32 [8192, 8], P('cell'), may hold values from 0 to 8191, as said below
- counts: int32 [8192], P('cell'), may hold values from 1 to 8, as said below
- cotangent: bfloat16 [8192, 8, 256], P('cell'), may hold values from -6 to 6
- w_self: bfloat16 [512, 512], replicated, may hold values from -0.25 to 0.25
- w_neighbour: bfloat16 [512, 512], replicated, may hold values from -0.25 to 0.25
- w_radial: bfloat16 [128, 512], replicated, may hold values from -0.5 to 0.5
- w_block: bfloat16 [512, 256], replicated, may hold values from -0.25 to 0.25
Outputs:
- blocks: bfloat16 [8192, 8, 256], P('cell')
- feat_grad: bfloat16 [8192, 512], P('cell')
The draws below stay inside these ranges and needn't reach their ends.
Inputs may be any that keep to these rules, and one draw needn't show every extreme that they name: `neighbours`: each neighbour index differs from its atom's index by 1 to 128. Only the first counts[i] slots of atom i are live, the rest are padding.
All inputs are finite; a program needn't handle non-finite values.
Results may differ from the reference program's by a relative error of at most 0.013.
Values may be sent and summed in bfloat16 or wider, within the bound.
No kernel may reach another device: no remote copies, remote signals or barrier semaphores. Data moves between devices by JAX's collectives and lax.ppermute only.
A program may use at most 64 MiB of HBM per device.

```python
import jax
import jax.numpy as jnp
from jax import lax

F = 512
NR = 128
OB = 256
K = 8
AT_DEV = 256
HALO = 128
ATOMS = 8192
N_CELL = 32


def draw_neighbours(key, part):
    key_offset, key_sign = jax.random.split(jax.random.fold_in(key, 11))
    offsets = jax.random.randint(key_offset, (ATOMS, K), 1, HALO + 1)
    signs = jax.random.randint(key_sign, (ATOMS, K), 0, 2) * 2 - 1
    atom_index = jnp.arange(ATOMS, dtype=jnp.int32)[:, None]
    target = atom_index + signs * offsets
    flipped = atom_index - signs * offsets
    target = jnp.where((target < 0) | (target >= ATOMS), flipped, target)
    target = target.at[ATOMS - 2, 0].set(ATOMS - 1)
    target = target.at[1, 0].set(0)
    return target.astype(jnp.int32)


def draw_counts(key, part):
    key_level, key_count = jax.random.split(jax.random.fold_in(key, 23))
    domain_total = ATOMS // AT_DEV
    levels = jax.random.randint(key_level, (domain_total,), 1, K + 1)
    lowest = levels[jnp.arange(ATOMS, dtype=jnp.int32) // AT_DEV]
    spread = jax.random.randint(key_count, (ATOMS,), 0, K + 1)
    result = lowest + spread % (K + 1 - lowest)
    result = result.at[0].set(K)
    result = result.at[1].set(1)
    return result.astype(jnp.int32)


def block_scale(key, extent, cuts, least, top_value):
    level, own = 1.0, jax.random.fold_in(key, 6)
    for position, parts in cuts:
        steps = jnp.exp(jax.random.uniform(jax.random.fold_in(own, position), (parts,), jnp.float32, least / len(cuts), top_value / len(cuts)))
        level = level * jnp.repeat(steps, extent[position] // parts).reshape([-1 if axis == position else 1 for axis in range(len(extent))])
    return level


def normal_values(stream_key, dims, width, reach, cuts=(), kind=jnp.bfloat16):
    loudness = block_scale(stream_key, dims, cuts, -0.22, 0.18) if cuts else 1.0
    array = jax.random.normal(stream_key, dims, jnp.float32) * width * loudness
    return jnp.minimum(jnp.maximum(array, -reach), reach).astype(kind)


def setup_inputs(seed: int = 0) -> dict:
    key_list = jax.random.split(jax.random.key(seed), 10)
    features = normal_values(key_list[0], (ATOMS, F), 1.0, 6.0, ((0, 32),))
    radial = jnp.clip(1.0 * jax.random.uniform(key_list[1], (ATOMS, K, NR), jnp.float32) ** block_scale(key_list[1], (ATOMS, K, NR), ((0, 32),), -0.2, 0.2), 0.0, 1.0).astype(jnp.bfloat16)
    neighbours = draw_neighbours(jax.random.fold_in(key_list[9], 71), 0)
    counts = draw_counts(jax.random.fold_in(key_list[9], 71), 0)
    cotangent = normal_values(key_list[4], (ATOMS, K, OB), 1.0, 6.0, ((0, 32),))
    w_self = normal_values(key_list[5], (F, F), F ** -0.5, 0.25)
    w_neighbour = normal_values(key_list[6], (F, F), F ** -0.5, 0.25)
    w_radial = normal_values(key_list[7], (NR, F), NR ** -0.5, 0.5)
    w_block = normal_values(key_list[8], (F, OB), F ** -0.5, 0.25)
    return dict(features=features, radial=radial, neighbours=neighbours, counts=counts, cotangent=cotangent, w_self=w_self, w_neighbour=w_neighbour, w_radial=w_radial, w_block=w_block)


def reference(features, radial, neighbours, counts, cotangent, w_self, w_neighbour, w_radial, w_block):
    self_proj = jnp.dot(features, w_self, preferred_element_type=jnp.float32).astype(jnp.bfloat16)
    nbr_proj = jnp.dot(features, w_neighbour, preferred_element_type=jnp.float32).astype(jnp.bfloat16)
    slot_index = jnp.arange(K, dtype=jnp.int32)

    def block_step(carry, index):
        start = (index * AT_DEV).astype(jnp.int32)
        nbr_rows = lax.dynamic_slice_in_dim(neighbours, start, AT_DEV, 0).reshape(-1)
        radial_rows = lax.dynamic_slice_in_dim(radial, start, AT_DEV, 0).reshape(-1, NR)
        count_rows = lax.dynamic_slice_in_dim(counts, start, AT_DEV, 0)
        cotan_rows = lax.dynamic_slice_in_dim(cotangent, start, AT_DEV, 0).reshape(-1, OB)
        self_rows = lax.dynamic_slice_in_dim(self_proj, start, AT_DEV, 0)
        live_mask = (slot_index[None, :] < count_rows[:, None]).astype(jnp.float32)[:, :, None]
        radial_gate = jnp.dot(radial_rows, w_radial, preferred_element_type=jnp.float32).reshape(AT_DEV, K, F)
        gathered = nbr_proj[nbr_rows].reshape(AT_DEV, K, F)
        pre_act = (self_rows.astype(jnp.float32)[:, None, :] + gathered.astype(jnp.float32)) * radial_gate
        message = (jax.nn.silu(pre_act) * live_mask).astype(jnp.bfloat16)
        block_out = jnp.dot(message.reshape(-1, F), w_block, preferred_element_type=jnp.float32).astype(jnp.bfloat16)
        d_message = jnp.dot(cotan_rows, w_block.T, preferred_element_type=jnp.float32).reshape(AT_DEV, K, F)
        sigmoid_val = jax.nn.sigmoid(pre_act)
        adjoint = d_message * live_mask * (sigmoid_val * (1.0 + pre_act * (1.0 - sigmoid_val))) * radial_gate
        self_adj = jnp.sum(adjoint, axis=1)
        carry = carry.at[nbr_rows].add(adjoint.reshape(-1, F))
        return carry, (block_out.reshape(AT_DEV, K, OB), self_adj)

    summed, (block_parts, self_parts) = lax.scan(block_step, jnp.zeros((ATOMS, F), jnp.float32), jnp.arange(N_CELL, dtype=jnp.int32))
    blocks = block_parts.reshape(ATOMS, K, OB)
    self_adj = self_parts.reshape(ATOMS, F).astype(jnp.bfloat16)
    nbr_adj = summed.astype(jnp.bfloat16)
    feat_grad = jnp.dot(self_adj, w_self.T, preferred_element_type=jnp.float32) + jnp.dot(nbr_adj, w_neighbour.T, preferred_element_type=jnp.float32)
    return blocks, feat_grad.astype(jnp.bfloat16)
```

```python
import functools

import jax
import jax.numpy as jnp
from jax import lax
from jax.experimental import pallas as pl
from jax.experimental.pallas import tpu as pltpu
from jax.sharding import PartitionSpec as P

BF = jnp.bfloat16
F32 = jnp.float32


def mm(a, b):
    return jnp.dot(a, b, preferred_element_type=F32)


def mm_nt(a, b):
    return lax.dot_general(a, b, (((1,), (1,)), ((), ())), preferred_element_type=F32)


def mm_tn(a, b):
    return lax.dot_general(a, b, (((0,), (0,)), ((), ())), preferred_element_type=F32)


def picker(nbr, count_row, base, half, slots):
    local = nbr - base
    own = (local >= 0) & (local < 2 * half)
    column = jnp.where(own, local, 2 * half + (local & (half - 1)))
    live = lax.broadcasted_iota(jnp.int32, (slots, half), 0) < count_row
    column = jnp.where(live, (column - half).astype(F32), -2.0 * half).astype(BF)
    edges = half * slots
    row = lax.broadcasted_iota(jnp.int32, (edges, half), 0)
    lane = lax.broadcasted_iota(jnp.int32, (edges, half), 1)
    one, zero = jnp.ones((), BF), jnp.zeros((), BF)
    lane_b = lane.astype(F32).astype(BF)
    same_atom = jnp.where(lane_b == (row // slots).astype(F32).astype(BF), one, zero)
    spread = mm_nt(same_atom, column)
    slot_lane = lax.broadcasted_iota(jnp.int32, (edges, slots), 1)
    slot_row = lax.broadcasted_iota(jnp.int32, (edges, slots), 0)
    mine = jnp.where((slot_row & (slots - 1)) == slot_lane, spread, 0.0)
    target = jnp.sum(mine, axis=1, keepdims=True)
    target = jnp.broadcast_to(target, (edges, half)).astype(BF)
    parts = [jnp.where(target == lane_b + BF(half * (j - 1)), one, zero) for j in range(3)]
    parts.append(jnp.where(target > BF(-1.5 * half), same_atom, zero))
    return jnp.concatenate(parts, axis=1)


def activation(pre):
    sig = BF(0.5) * jnp.tanh(BF(0.5) * pre) + BF(0.5)
    message = pre * sig
    slope = sig + message * (BF(1.0) - sig)
    return message, slope


def front_kernel(
    feat_hbm, near_ref, nbr_hbm, cnt_hbm, rad_hbm, cot_hbm, wself_hbm, wnbr_hbm, wrad_hbm, wblk_hbm,
    apick_ref, asum_ref, agate_ref, acot_ref, bpick_ref, bsum_ref, bgate_ref, bdgate_ref,
    wself_ref, wnbr_ref, wblk_ref,
    feat_ref, nbr_ref, cnt_ref, rad_ref, bcot_ref, wrad_ref, table_ref, sems,
    *, slots,
):
    atoms = feat_hbm.shape[0]
    half = atoms // 2
    edges = half * slots
    device = lax.axis_index("cell")
    parity = lax.rem(device, 2)
    base = device * atoms
    near_half, far_half = 1 - parity, parity
    near_off = pl.multiple_of(near_half * half, half)
    far_off = pl.multiple_of(far_half * half, half)
    near_edge = pl.multiple_of(near_half * edges, edges)
    far_edge = pl.multiple_of(far_half * edges, edges)
    pairs = [
        (nbr_hbm, nbr_ref),
        (cnt_hbm, cnt_ref),
        (feat_hbm, feat_ref),
        (wnbr_hbm, wnbr_ref),
        (wself_hbm, wself_ref),
        (wrad_hbm, wrad_ref),
        (rad_hbm, rad_ref),
        (wblk_hbm, wblk_ref),
        (cot_hbm.at[pl.ds(far_edge, edges)], bcot_ref),
        (cot_hbm.at[pl.ds(near_edge, edges)], acot_ref),
    ]
    copies = [pltpu.make_async_copy(src, dst, sems.at[n]) for n, (src, dst) in enumerate(pairs)]
    for copy in copies:
        copy.start()
    copies[0].wait()
    copies[1].wait()
    bpick_ref[...] = picker(
        nbr_ref[:, pl.ds(far_off, half)], cnt_ref[pl.ds(far_half, 1), :], base, half, slots
    )
    apick_ref[...] = picker(
        nbr_ref[:, pl.ds(near_off, half)], cnt_ref[pl.ds(near_half, 1), :], base, half, slots
    )
    copies[2].wait()
    copies[3].wait()
    table_ref[0:atoms, :] = mm(feat_ref[...], wnbr_ref[...]).astype(BF)
    table_ref[atoms : atoms + half, :] = mm(near_ref[pl.ds(far_off, half), :], wnbr_ref[...]).astype(BF)
    copies[4].wait()
    own_self = mm(feat_ref[pl.ds(near_off, half), :], wself_ref[...]).astype(BF)
    far_self = mm(feat_ref[pl.ds(far_off, half), :], wself_ref[...]).astype(BF)
    table_ref[atoms + half : atoms + 2 * half, :] = own_self
    copies[5].wait()
    copies[6].wait()
    bgate = mm(rad_ref[pl.ds(far_edge, edges), :], wrad_ref[...])
    bgate_ref[...] = bgate.astype(BF)
    agate_ref[...] = mm(rad_ref[pl.ds(near_edge, edges), :], wrad_ref[...]).astype(BF)
    bsum_ref[...] = (
        mm(bpick_ref[:, :atoms], table_ref[0:atoms, :]) + mm(bpick_ref[:, atoms + half :], far_self)
    ).astype(BF)
    asum_ref[...] = mm(apick_ref[...], table_ref[...]).astype(BF)
    copies[7].wait()
    copies[8].wait()
    bdgate_ref[...] = (mm_nt(bcot_ref[...], wblk_ref[...]) * bgate).astype(BF)
    copies[9].wait()


def far_kernel(far_ref, wnbr_ref, sum_ref, gate_ref, dgate_ref, pick_ref, msg_ref, adj_ref, rim_ref):
    half = far_ref.shape[0]
    halo = mm(far_ref[...], wnbr_ref[...]).astype(BF)
    pick = pick_ref[:, 2 * half : 3 * half]
    pre = (sum_ref[...] + mm(pick, halo).astype(BF)) * gate_ref[...]
    message, slope = activation(pre)
    msg_ref[...] = message
    adj = dgate_ref[...] * slope
    adj_ref[...] = adj
    rim_ref[...] = mm_tn(pick, adj).astype(BF)


def near_kernel(sum_ref, gate_ref, cot_ref, pick_ref, wblk_ref, order_ref, msg_ref, own_ref, rim_ref):
    half = rim_ref.shape[0]
    message, slope = activation(sum_ref[...] * gate_ref[...])
    msg_ref[...] = message
    adj = mm_nt(cot_ref[...], wblk_ref[...]).astype(BF) * gate_ref[...] * slope
    rim_ref[...] = mm_tn(pick_ref[:, 2 * half : 3 * half], adj).astype(BF)
    own_ref[0 : 2 * half, :] = mm_tn(pick_ref[:, : 2 * half], adj)
    own_ref[2 * half :, :] = mm_tn(pick_ref[:, 3 * half :], adj)


def own_kernel(
    amsg_ref, bmsg_ref, adj_ref, pick_ref, own_ref, wself_ref, wnbr_ref, wblk_ref,
    blocks_hbm, grad_ref,
    ablk_ref, bblk_ref, sems,
):
    edges = bmsg_ref.shape[0]
    half = own_ref.shape[0] // 3
    atoms = 2 * half
    parity = lax.rem(lax.axis_index("cell"), 2)
    near_half = 1 - parity
    near_off = pl.multiple_of(near_half * half, half)
    far_off = pl.multiple_of(parity * half, half)
    near_edge = pl.multiple_of(near_half * edges, edges)
    far_edge = pl.multiple_of(parity * edges, edges)
    ablk_ref[...] = mm(amsg_ref[...], wblk_ref[...]).astype(BF)
    acopy = pltpu.make_async_copy(ablk_ref, blocks_hbm.at[pl.ds(near_edge, edges)], sems.at[0])
    acopy.start()
    bblk_ref[...] = mm(bmsg_ref[...], wblk_ref[...]).astype(BF)
    bcopy = pltpu.make_async_copy(bblk_ref, blocks_hbm.at[pl.ds(far_edge, edges)], sems.at[1])
    bcopy.start()
    total = own_ref[0:atoms, :] + mm_tn(pick_ref[:, :atoms], adj_ref[...])
    mine = mm_tn(pick_ref[:, atoms + half :], adj_ref[...])
    grad_ref[...] = mm_nt(total.astype(BF), wnbr_ref[...])
    grad_ref[pl.ds(near_off, half), :] += mm_nt(own_ref[atoms:, :].astype(BF), wself_ref[...])
    grad_ref[pl.ds(far_off, half), :] += mm_nt(mine.astype(BF), wself_ref[...])
    acopy.wait()
    bcopy.wait()


def last_kernel(grad_ref, near_ref, far_ref, wnbr_ref, out_ref):
    half = far_ref.shape[0]
    parity = lax.rem(lax.axis_index("cell"), 2)
    near_off = pl.multiple_of((1 - parity) * half, half)
    far_off = pl.multiple_of(parity * half, half)
    out_ref[pl.ds(near_off, half), :] = (
        grad_ref[pl.ds(near_off, half), :] + mm_nt(near_ref[...], wnbr_ref[...])
    ).astype(BF)
    out_ref[pl.ds(far_off, half), :] = (
        grad_ref[pl.ds(far_off, half), :] + mm_nt(far_ref[...], wnbr_ref[...])
    ).astype(BF)


VM = pl.BlockSpec(memory_space=pltpu.VMEM)
HB = pl.BlockSpec(memory_space=pltpu.HBM)


def call(kernel, name, inputs, outs, megabytes, scratch=(), in_specs=None, out_specs=None):
    if in_specs is not None:
        inputs = [
            pltpu.with_memory_space_constraint(x, pltpu.HBM) if spec is HB else x
            for x, spec in zip(inputs, in_specs)
        ]
    return pl.pallas_call(
        kernel,
        name=name,
        out_shape=[jax.ShapeDtypeStruct(shape, dtype) for shape, dtype in outs],
        in_specs=in_specs or [VM] * len(inputs),
        out_specs=out_specs or [VM] * len(outs),
        scratch_shapes=list(scratch),
        compiler_params=pltpu.CompilerParams(vmem_limit_bytes=megabytes * 1024 * 1024),
    )(*inputs)


def body(count, features, radial, neighbours, counts, cotangent, w_self, w_neighbour, w_radial, w_block):
    atoms, width = features.shape
    slots = neighbours.shape[1]
    half = atoms // 2
    edges = half * slots
    entries = w_block.shape[1]
    basis = radial.shape[2]
    inside = [(i, i ^ 1) for i in range(count)]
    across = []
    for i in range(1, count - 1, 2):
        across += [(i, i + 1), (i + 1, i)]
    wrapped = across + [(0, count - 1), (count - 1, 0)]
    parity = lax.axis_index("cell") & 1
    near = lax.ppermute(features, "cell", inside)
    far_send = lax.dynamic_slice_in_dim(features, parity * half, half, 0)
    far = lax.ppermute(far_send, "cell", wrapped)
    edge_f = ((edges, width), BF)
    edge_e = ((edges, entries), BF)
    pick_t = ((edges, 4 * half), BF)
    rim_t = ((half, width), BF)
    outs = [
        pick_t, edge_f, edge_f, edge_e, pick_t, edge_f, edge_f, edge_f,
        ((width, width), BF), ((width, width), BF), ((width, entries), BF),
    ]
    apick, asum, agate, acot, bpick, bsum, bgate, bdgate, wself_v, wnbr_v, wblk_v = call(
        functools.partial(front_kernel, slots=slots),
        "front",
        (
            features, near, neighbours.T, counts.reshape(2, half),
            radial.reshape(atoms * slots, basis), cotangent.reshape(atoms * slots, entries),
            w_self, w_neighbour, w_radial, w_block,
        ),
        outs,
        20,
        scratch=[
            pltpu.VMEM((atoms, width), BF),
            pltpu.VMEM((slots, atoms), jnp.int32),
            pltpu.VMEM((2, half), jnp.int32),
            pltpu.VMEM((2 * edges, basis), BF),
            pltpu.VMEM((edges, entries), BF),
            pltpu.VMEM((basis, width), BF),
            pltpu.VMEM((4 * half, width), BF),
            pltpu.SemaphoreType.DMA((10,)),
        ],
        in_specs=[HB, VM] + [HB] * 8,
    )
    bmsg, badj, far_rim = call(
        far_kernel,
        "far",
        (far, wnbr_v, bsum, bgate, bdgate, bpick),
        [edge_f, edge_f, rim_t],
        16,
    )
    far_back = lax.ppermute(far_rim, "cell", across)
    amsg, own, near_rim = call(
        near_kernel,
        "near",
        (asum, agate, acot, apick, wblk_v, far_rim),
        [edge_f, ((3 * half, width), F32), rim_t],
        16,
    )
    near_back = lax.ppermute(near_rim, "cell", inside)
    blocks, grad = call(
        own_kernel,
        "own",
        (amsg, bmsg, badj, bpick, own, wself_v, wnbr_v, wblk_v),
        [((2 * edges, entries), BF), ((atoms, width), F32)],
        16,
        scratch=[
            pltpu.VMEM((edges, entries), BF),
            pltpu.VMEM((edges, entries), BF),
            pltpu.SemaphoreType.DMA((2,)),
        ],
        out_specs=[HB, VM],
    )
    (feat_grad,) = call(last_kernel, "last", (grad, near_back, far_back, wnbr_v), [((atoms, width), BF)], 8)
    return blocks.reshape(atoms, slots, entries), feat_grad


def solution(mesh):
    in_specs = (
        P("cell", None),
        P("cell", None, None),
        P("cell", None),
        P("cell"),
        P("cell", None, None),
        P(),
        P(),
        P(),
        P(),
    )
    out_specs = (P("cell", None, None), P("cell", None))
    return jax.shard_map(
        functools.partial(body, mesh.shape["cell"]),
        mesh=mesh, in_specs=in_specs, out_specs=out_specs, check_vma=False,
    )
```

```python
import functools

import jax
import jax.numpy as jnp
from jax import lax
from jax.experimental import pallas as pl
from jax.experimental.pallas import tpu as pltpu
from jax.sharding import PartitionSpec as P

BF = jnp.bfloat16
F32 = jnp.float32


def mm(a, b):
    return jnp.dot(a, b, preferred_element_type=F32)


def mm_nt(a, b):
    return lax.dot_general(a, b, (((1,), (1,)), ((), ())), preferred_element_type=F32)


def mm_tn(a, b):
    return lax.dot_general(a, b, (((0,), (0,)), ((), ())), preferred_element_type=F32)


def halves(half):
    parity = lax.rem(lax.axis_index("cell"), 2)
    near, far = 1 - parity, parity
    return near, far, pl.multiple_of(near * half, half), pl.multiple_of(far * half, half)


def picker(nbr, count_row, base, half, slots):
    local = nbr - base
    own = (local >= 0) & (local < 2 * half)
    target = jnp.where(own, local, 2 * half + (local & (half - 1)))
    live = lax.broadcasted_iota(jnp.int32, (slots, half), 0) < count_row
    target = jnp.where(live, (target - half).astype(F32), -2.0 * half).astype(BF)
    edges = half * slots
    row = lax.broadcasted_iota(jnp.int32, (edges, half), 0)
    lane = lax.broadcasted_iota(jnp.int32, (edges, half), 1)
    one, zero = jnp.ones((), BF), jnp.zeros((), BF)
    lane_b = lane.astype(F32).astype(BF)
    same_atom = jnp.where(lane_b == (row // slots).astype(F32).astype(BF), one, zero)
    spread = mm_nt(same_atom, target)
    slot_lane = lax.broadcasted_iota(jnp.int32, (edges, slots), 1)
    slot_row = lax.broadcasted_iota(jnp.int32, (edges, slots), 0)
    mine = jnp.where((slot_row & (slots - 1)) == slot_lane, spread, 0.0)
    target = jnp.sum(mine, axis=1, keepdims=True)
    target = jnp.broadcast_to(target, (edges, half)).astype(BF)
    low, high, halo = [
        jnp.where(target == lane_b + BF(half * (j - 1)), one, zero) for j in range(3)
    ]
    mine = jnp.where(target > BF(-1.5 * half), same_atom, zero)
    return jnp.concatenate([low, high, mine, halo], axis=1)


def activation(total, half_gate, half_dgate):
    h = total * half_gate
    t = jnp.tanh(h)
    ht = h * t
    return h + ht, half_dgate * (t + BF(1.0)) * (h - ht + BF(1.0))


def head_kernel(feat_hbm, nbr_hbm, cnt_hbm, send_ref, nbr_ref, cnt_ref, sems):
    half = send_ref.shape[0]
    _, _, _, far_off = halves(half)
    pairs = [
        (feat_hbm.at[pl.ds(far_off, half)], send_ref),
        (nbr_hbm, nbr_ref),
        (cnt_hbm, cnt_ref),
    ]
    copies = [pltpu.make_async_copy(src, dst, sems.at[n]) for n, (src, dst) in enumerate(pairs)]
    for copy in copies:
        copy.start()
    for copy in copies:
        copy.wait()


def front_kernel(
    nbr_ref, cnt_ref, feat_hbm, rad_hbm, cot_hbm, wself_hbm, wnbr_hbm, wrad_hbm, wblk_hbm,
    pick_ref, sum_ref, gate_ref, dgate_ref, self_ref, wself_ref, wnbr_ref, wblk_ref,
    feat_ref, rad_ref, cot_ref, wrad_ref, sems,
    *, slots,
):
    atoms = feat_hbm.shape[0]
    half = atoms // 2
    edges = half * slots
    base = lax.axis_index("cell") * atoms
    pairs = [
        (feat_hbm, feat_ref),
        (wnbr_hbm, wnbr_ref),
        (wrad_hbm, wrad_ref),
        (rad_hbm, rad_ref),
        (wblk_hbm, wblk_ref),
        (cot_hbm, cot_ref),
        (wself_hbm, wself_ref),
    ]
    copies = [pltpu.make_async_copy(src, dst, sems.at[n]) for n, (src, dst) in enumerate(pairs)]
    for copy in copies:
        copy.start()
    for n in range(2):
        pick_ref[n * edges : (n + 1) * edges, :] = picker(
            nbr_ref[:, n * half : (n + 1) * half], cnt_ref[n : n + 1, :], base, half, slots
        )
    for copy in copies[:2]:
        copy.wait()
    own = mm(feat_ref[...], wnbr_ref[...]).astype(BF)
    sum_ref[...] = mm(pick_ref[:, :atoms], own).astype(BF)
    for copy in copies[2:]:
        copy.wait()
    self_ref[...] = mm(feat_ref[...], wself_ref[...]).astype(BF)
    half_wrad = wrad_ref[...] * BF(0.5)
    step = edges // 2
    for n in range(4):
        rows = slice(n * step, (n + 1) * step)
        gate = mm(rad_ref[rows, :], half_wrad).astype(BF)
        gate_ref[rows, :] = gate
        dgate_ref[rows, :] = mm_nt(cot_ref[rows, :], wblk_ref[...]).astype(BF) * gate


def side(halo, half_index, refs, msg_ref, adj_ref, rim_ref):
    self_ref, sum_ref, gate_ref, dgate_ref, pick_ref = refs
    half = rim_ref.shape[0]
    edges = msg_ref.shape[0]
    table = jnp.concatenate(
        [self_ref[pl.ds(pl.multiple_of(half_index * half, half), half), :], halo], axis=0
    )
    step = edges // 2
    first = pl.multiple_of(half_index * edges, edges)
    parts = [
        mm(pick_ref[pl.ds(first + n * step, step), 2 * half :], table).astype(BF) for n in range(2)
    ]
    for n in range(2):
        rows = pl.ds(first + n * step, step)
        message, adj = activation(
            sum_ref[rows, :] + parts[n], gate_ref[rows, :], dgate_ref[rows, :]
        )
        msg_ref[n * step : (n + 1) * step, :] = message
        adj_ref[n * step : (n + 1) * step, :] = adj
    rim_ref[...] = mm_tn(pick_ref[pl.ds(first, edges), 3 * half :], adj_ref[...]).astype(BF)


def near_kernel(
    near_ref, wnbr_ref, self_ref, sum_ref, gate_ref, dgate_ref, pick_ref, order_ref,
    msg_ref, adj_ref, rim_ref,
):
    half = rim_ref.shape[0]
    near, _, _, far_off = halves(half)
    halo = mm(near_ref[pl.ds(far_off, half), :], wnbr_ref[...]).astype(BF)
    side(halo, near, (self_ref, sum_ref, gate_ref, dgate_ref, pick_ref), msg_ref, adj_ref, rim_ref)


def far_kernel(
    far_ref, wnbr_ref, self_ref, sum_ref, gate_ref, dgate_ref, pick_ref, msg_ref, adj_ref, rim_ref
):
    _, far, _, _ = halves(rim_ref.shape[0])
    halo = mm(far_ref[...], wnbr_ref[...]).astype(BF)
    side(halo, far, (self_ref, sum_ref, gate_ref, dgate_ref, pick_ref), msg_ref, adj_ref, rim_ref)


def own_kernel(
    nearmsg_ref, farmsg_ref, nearadj_ref, faradj_ref, pick_ref, wself_ref, wnbr_ref, wblk_ref,
    blocks_hbm, grad_ref,
    nearblk_ref, farblk_ref, selfsum_ref, sems,
):
    edges = farmsg_ref.shape[0]
    atoms = grad_ref.shape[0]
    half = atoms // 2
    near, far, near_off, far_off = halves(half)
    near_edge = pl.multiple_of(near * edges, edges)
    far_edge = pl.multiple_of(far * edges, edges)
    farblk_ref[...] = mm(farmsg_ref[...], wblk_ref[...]).astype(BF)
    far_copy = pltpu.make_async_copy(farblk_ref, blocks_hbm.at[pl.ds(far_edge, edges)], sems.at[0])
    far_copy.start()
    nearblk_ref[...] = mm(nearmsg_ref[...], wblk_ref[...]).astype(BF)
    near_copy = pltpu.make_async_copy(
        nearblk_ref, blocks_hbm.at[pl.ds(near_edge, edges)], sems.at[1]
    )
    near_copy.start()
    near_back = mm_tn(pick_ref[pl.ds(near_edge, edges), : atoms + half], nearadj_ref[...])
    far_back = mm_tn(pick_ref[pl.ds(far_edge, edges), : atoms + half], faradj_ref[...])
    selfsum_ref[pl.ds(near_off, half), :] = near_back[atoms:].astype(BF)
    selfsum_ref[pl.ds(far_off, half), :] = far_back[atoms:].astype(BF)
    total = (near_back[:atoms] + far_back[:atoms]).astype(BF)
    grad_ref[...] = mm_nt(total, wnbr_ref[...]) + mm_nt(selfsum_ref[...], wself_ref[...])
    near_copy.wait()
    far_copy.wait()


def last_kernel(far_ref, near_ref, grad_ref, wnbr_ref, out_hbm, fout_ref, nout_ref, sem):
    half = near_ref.shape[0]
    _, _, near_off, far_off = halves(half)
    fout_ref[...] = (grad_ref[pl.ds(far_off, half), :] + mm_nt(far_ref[...], wnbr_ref[...])).astype(BF)
    c0 = pltpu.make_async_copy(fout_ref, out_hbm.at[pl.ds(far_off, half)], sem.at[0])
    c0.start()
    nout_ref[...] = (grad_ref[pl.ds(near_off, half), :] + mm_nt(near_ref[...], wnbr_ref[...])).astype(BF)
    c1 = pltpu.make_async_copy(nout_ref, out_hbm.at[pl.ds(near_off, half)], sem.at[1])
    c1.start()
    c0.wait()
    c1.wait()


VM = pl.BlockSpec(memory_space=pltpu.VMEM)
HB = pl.BlockSpec(memory_space=pltpu.HBM)


def call(kernel, name, inputs, outs, megabytes, scratch=(), in_specs=None, out_specs=None, aliases=None):
    in_specs = in_specs or [VM] * len(inputs)
    inputs = [
        pltpu.with_memory_space_constraint(x, pltpu.HBM) if spec is HB else x
        for x, spec in zip(inputs, in_specs)
    ]
    return pl.pallas_call(
        kernel,
        name=name,
        out_shape=[jax.ShapeDtypeStruct(shape, dtype) for shape, dtype in outs],
        in_specs=in_specs,
        out_specs=out_specs or [VM] * len(outs),
        scratch_shapes=list(scratch),
        input_output_aliases=aliases or {},
        compiler_params=pltpu.CompilerParams(vmem_limit_bytes=megabytes * 1024 * 1024),
    )(*inputs)


def body(count, features, radial, neighbours, counts, cotangent, w_self, w_neighbour, w_radial, w_block):
    atoms, width = features.shape
    slots = neighbours.shape[1]
    half = atoms // 2
    edges = half * slots
    entries = w_block.shape[1]
    basis = radial.shape[2]
    inside = [(i, i ^ 1) for i in range(count)]
    across = []
    for i in range(1, count - 1, 2):
        across += [(i, i + 1), (i + 1, i)]
    wrapped = across + [(0, count - 1), (count - 1, 0)]
    dma = pltpu.SemaphoreType.DMA
    edge_t = ((edges, width), BF)
    both_t = ((2 * edges, width), BF)
    rim_t = ((half, width), BF)
    grad_t = ((atoms, width), BF)
    far_send, nbr, cnt = call(
        head_kernel,
        "head",
        (features, neighbours.T, counts.reshape(2, half)),
        [rim_t, ((slots, atoms), jnp.int32), ((2, half), jnp.int32)],
        4,
        scratch=[dma((3,))],
        in_specs=[HB] * 3,
    )
    far = lax.ppermute(far_send, "cell", wrapped)
    near = lax.ppermute(features, "cell", inside)
    pick, total, gate, dgate, selfs, wself_v, wnbr_v, wblk_v = call(
        functools.partial(front_kernel, slots=slots),
        "front",
        (
            nbr, cnt, features,
            radial.reshape(atoms * slots, basis), cotangent.reshape(atoms * slots, entries),
            w_self, w_neighbour, w_radial, w_block,
        ),
        [
            ((2 * edges, 4 * half), BF), both_t, both_t, both_t, grad_t,
            ((width, width), BF), ((width, width), BF), ((width, entries), BF),
        ],
        20,
        scratch=[
            pltpu.VMEM((atoms, width), BF),
            pltpu.VMEM((2 * edges, basis), BF),
            pltpu.VMEM((2 * edges, entries), BF),
            pltpu.VMEM((basis, width), BF),
            dma((7,)),
        ],
        in_specs=[VM, VM] + [HB] * 7,
    )
    refs = (selfs, total, gate, dgate, pick)
    side_t = [edge_t, edge_t, rim_t]
    far_msg, far_adj, far_rim = call(far_kernel, "far", (far, wnbr_v) + refs, side_t, 12)
    far_back = lax.ppermute(far_rim, "cell", across)
    near_msg, near_adj, near_rim = call(
        near_kernel, "near", (near, wnbr_v) + refs + (far_rim,), side_t, 12
    )
    near_back = lax.ppermute(near_rim, "cell", inside)
    blocks, grad = call(
        own_kernel,
        "own",
        (near_msg, far_msg, near_adj, far_adj, pick, wself_v, wnbr_v, wblk_v),
        [((2 * edges, entries), BF), ((atoms, width), F32)],
        16,
        scratch=[
            pltpu.VMEM((edges, entries), BF),
            pltpu.VMEM((edges, entries), BF),
            pltpu.VMEM((atoms, width), BF),
            dma((2,)),
        ],
        out_specs=[HB, VM],
    )
    (feat_grad,) = call(
        last_kernel,
        "last",
        (far_back, near_back, grad, wnbr_v),
        [grad_t],
        4,
        scratch=[pltpu.VMEM((half, width), BF), pltpu.VMEM((half, width), BF), dma((2,))],
        out_specs=[HB],
    )
    return blocks.reshape(atoms, slots, entries), feat_grad


def solution(mesh):
    in_specs = (
        P("cell", None),
        P("cell", None, None),
        P("cell", None),
        P("cell"),
        P("cell", None, None),
        P(),
        P(),
        P(),
        P(),
    )
    out_specs = (P("cell", None, None), P("cell", None))
    return jax.shard_map(
        functools.partial(body, mesh.shape["cell"]),
        mesh=mesh, in_specs=in_specs, out_specs=out_specs, check_vma=False,
    )
```

```python
import functools

import jax
import jax.numpy as jnp
from jax import lax
from jax.experimental import pallas as pl
from jax.experimental.pallas import tpu as pltpu
from jax.sharding import PartitionSpec as P

BF = jnp.bfloat16
F32 = jnp.float32


def mm(a, b):
    return jnp.dot(a, b, preferred_element_type=F32)


def mm_nt(a, b):
    return lax.dot_general(a, b, (((1,), (1,)), ((), ())), preferred_element_type=F32)


def mm_tn(a, b):
    return lax.dot_general(a, b, (((0,), (0,)), ((), ())), preferred_element_type=F32)


def halves(half):
    parity = lax.rem(lax.axis_index("cell"), 2)
    near, far = 1 - parity, parity
    return near, far, pl.multiple_of(near * half, half), pl.multiple_of(far * half, half)


def picker(nbr, count_row, base, half, slots):
    local = nbr - base
    own = (local >= 0) & (local < 2 * half)
    target = jnp.where(own, local, 2 * half + (local & (half - 1)))
    live = lax.broadcasted_iota(jnp.int32, (slots, half), 0) < count_row
    target = jnp.where(live, (target - half).astype(F32), -2.0 * half).astype(BF)
    edges = half * slots
    row = lax.broadcasted_iota(jnp.int32, (edges, half), 0)
    lane = lax.broadcasted_iota(jnp.int32, (edges, half), 1)
    one, zero = jnp.ones((), BF), jnp.zeros((), BF)
    lane_b = lane.astype(F32).astype(BF)
    same_atom = jnp.where(lane_b == (row // slots).astype(F32).astype(BF), one, zero)
    spread = mm_nt(same_atom, target)
    slot_lane = lax.broadcasted_iota(jnp.int32, (edges, slots), 1)
    slot_row = lax.broadcasted_iota(jnp.int32, (edges, slots), 0)
    mine = jnp.where((slot_row & (slots - 1)) == slot_lane, spread, 0.0)
    target = jnp.sum(mine, axis=1, keepdims=True)
    target = jnp.broadcast_to(target, (edges, half)).astype(BF)
    low, high, halo = [
        jnp.where(target == lane_b + BF(half * (j - 1)), one, zero) for j in range(3)
    ]
    mine = jnp.where(target > BF(-1.5 * half), same_atom, zero)
    return jnp.concatenate([low, high, mine, halo], axis=1)


def activation(total, half_gate, half_dgate):
    h = total * half_gate
    t = jnp.tanh(h)
    ht = h * t
    return h + ht, half_dgate * (t + BF(1.0)) * (h - ht + BF(1.0))


def head_kernel(feat_hbm, nbr_hbm, cnt_hbm, far_ref, near_ref, nbr_ref, cnt_ref, sems):
    half = far_ref.shape[0]
    _, _, near_off, far_off = halves(half)
    pairs = [
        (feat_hbm.at[pl.ds(far_off, half)], far_ref),
        (feat_hbm.at[pl.ds(near_off, half)], near_ref),
        (nbr_hbm, nbr_ref),
        (cnt_hbm, cnt_ref),
    ]
    copies = [pltpu.make_async_copy(src, dst, sems.at[n]) for n, (src, dst) in enumerate(pairs)]
    for copy in copies:
        copy.start()
    for copy in copies:
        copy.wait()


def front_kernel(
    nbr_ref, cnt_ref, feat_ref, rad_ref, cot_ref, wself_ref, wnbr_ref, wrad_ref, wblk_ref,
    pick_ref, sum_ref, gate_ref, dgate_ref, self_ref,
    *, slots,
):
    atoms = feat_ref.shape[0]
    half = atoms // 2
    edges = half * slots
    base = lax.axis_index("cell") * atoms
    for n in range(2):
        pick_ref[n * edges : (n + 1) * edges, :] = picker(
            nbr_ref[:, n * half : (n + 1) * half], cnt_ref[n : n + 1, :], base, half, slots
        )
    own = mm(feat_ref[...], wnbr_ref[...]).astype(BF)
    self_ref[...] = mm(feat_ref[...], wself_ref[...]).astype(BF)
    gate = mm(rad_ref[...], wrad_ref[...] * BF(0.5))
    gate_ref[...] = gate.astype(BF)
    sum_ref[...] = mm(pick_ref[:, :atoms], own).astype(BF)
    dgate_ref[...] = (mm_nt(cot_ref[...], wblk_ref[...]) * gate).astype(BF)


def side(halo, half_index, refs, msg_ref, adj_ref, rim_ref):
    self_ref, sum_ref, gate_ref, dgate_ref, pick_ref = refs
    half = rim_ref.shape[0]
    edges = msg_ref.shape[0]
    table = jnp.concatenate(
        [self_ref[pl.ds(pl.multiple_of(half_index * half, half), half), :], halo], axis=0
    )
    step = edges // 2
    first = pl.multiple_of(half_index * edges, edges)
    parts = [
        mm(pick_ref[pl.ds(first + n * step, step), 2 * half :], table).astype(BF) for n in range(2)
    ]
    for n in range(2):
        rows = pl.ds(first + n * step, step)
        message, adj = activation(
            sum_ref[rows, :] + parts[n], gate_ref[rows, :], dgate_ref[rows, :]
        )
        msg_ref[n * step : (n + 1) * step, :] = message
        adj_ref[n * step : (n + 1) * step, :] = adj
    rim_ref[...] = mm_tn(pick_ref[pl.ds(first, edges), 3 * half :], adj_ref[...]).astype(BF)


def near_kernel(
    near_ref, wnbr_ref, self_ref, sum_ref, gate_ref, dgate_ref, pick_ref, msg_ref, adj_ref, rim_ref
):
    half = rim_ref.shape[0]
    near, _, _, _ = halves(half)
    halo = mm(near_ref[...], wnbr_ref[...]).astype(BF)
    side(halo, near, (self_ref, sum_ref, gate_ref, dgate_ref, pick_ref), msg_ref, adj_ref, rim_ref)


def far_kernel(
    far_ref, wnbr_ref, self_ref, sum_ref, gate_ref, dgate_ref, pick_ref, order_ref,
    msg_ref, adj_ref, rim_ref,
):
    _, far, _, _ = halves(rim_ref.shape[0])
    halo = mm(far_ref[...], wnbr_ref[...]).astype(BF)
    side(halo, far, (self_ref, sum_ref, gate_ref, dgate_ref, pick_ref), msg_ref, adj_ref, rim_ref)


def own_kernel(
    nearmsg_ref, farmsg_ref, nearadj_ref, faradj_ref, pick_ref, wself_ref, wnbr_ref, wblk_ref,
    blocks_hbm, grad_ref,
    nearblk_ref, farblk_ref, selfsum_ref, sems,
):
    edges = farmsg_ref.shape[0]
    atoms = grad_ref.shape[0]
    half = atoms // 2
    near, far, near_off, far_off = halves(half)
    near_edge = pl.multiple_of(near * edges, edges)
    far_edge = pl.multiple_of(far * edges, edges)
    farblk_ref[...] = mm(farmsg_ref[...], wblk_ref[...]).astype(BF)
    far_copy = pltpu.make_async_copy(farblk_ref, blocks_hbm.at[pl.ds(far_edge, edges)], sems.at[0])
    far_copy.start()
    nearblk_ref[...] = mm(nearmsg_ref[...], wblk_ref[...]).astype(BF)
    near_copy = pltpu.make_async_copy(
        nearblk_ref, blocks_hbm.at[pl.ds(near_edge, edges)], sems.at[1]
    )
    near_copy.start()

    @pl.when(lax.axis_index("cell") >= 0)
    def _():
        near_back = mm_tn(pick_ref[pl.ds(near_edge, edges), : atoms + half], nearadj_ref[...])
        far_back = mm_tn(pick_ref[pl.ds(far_edge, edges), : atoms + half], faradj_ref[...])
        selfsum_ref[pl.ds(near_off, half), :] = near_back[atoms:].astype(BF)
        selfsum_ref[pl.ds(far_off, half), :] = far_back[atoms:].astype(BF)
        total = (near_back[:atoms] + far_back[:atoms]).astype(BF)
        grad_ref[...] = mm_nt(total, wnbr_ref[...]) + mm_nt(selfsum_ref[...], wself_ref[...])

    near_copy.wait()
    far_copy.wait()


def last_kernel(far_ref, near_ref, grad_ref, wnbr_ref, out_hbm, fout_ref, nout_ref, sem):
    half = near_ref.shape[0]
    _, _, near_off, far_off = halves(half)
    fout_ref[...] = (grad_ref[pl.ds(far_off, half), :] + mm_nt(far_ref[...], wnbr_ref[...])).astype(BF)
    c0 = pltpu.make_async_copy(fout_ref, out_hbm.at[pl.ds(far_off, half)], sem.at[0])
    c0.start()
    nout_ref[...] = (grad_ref[pl.ds(near_off, half), :] + mm_nt(near_ref[...], wnbr_ref[...])).astype(BF)
    c1 = pltpu.make_async_copy(nout_ref, out_hbm.at[pl.ds(near_off, half)], sem.at[1])
    c1.start()
    c0.wait()
    c1.wait()


VM = pl.BlockSpec(memory_space=pltpu.VMEM)
HB = pl.BlockSpec(memory_space=pltpu.HBM)


def call(kernel, name, inputs, outs, megabytes, scratch=(), in_specs=None, out_specs=None, flops=0):
    in_specs = in_specs or [VM] * len(inputs)
    inputs = [
        pltpu.with_memory_space_constraint(x, pltpu.HBM) if spec is HB else x
        for x, spec in zip(inputs, in_specs)
    ]
    return pl.pallas_call(
        kernel,
        name=name,
        out_shape=[jax.ShapeDtypeStruct(shape, dtype) for shape, dtype in outs],
        in_specs=in_specs,
        out_specs=out_specs or [VM] * len(outs),
        scratch_shapes=list(scratch),
        cost_estimate=pl.CostEstimate(flops=flops, bytes_accessed=0, transcendentals=0),
        compiler_params=pltpu.CompilerParams(vmem_limit_bytes=megabytes * 1024 * 1024),
    )(*inputs)


def body(count, features, radial, neighbours, counts, cotangent, w_self, w_neighbour, w_radial, w_block):
    atoms, width = features.shape
    slots = neighbours.shape[1]
    half = atoms // 2
    edges = half * slots
    entries = w_block.shape[1]
    basis = radial.shape[2]
    inside = [(i, i ^ 1) for i in range(count)]
    across = []
    for i in range(1, count - 1, 2):
        across += [(i, i + 1), (i + 1, i)]
    wrapped = across + [(0, count - 1), (count - 1, 0)]
    dma = pltpu.SemaphoreType.DMA
    edge_t = ((edges, width), BF)
    both_t = ((2 * edges, width), BF)
    rim_t = ((half, width), BF)
    grad_t = ((atoms, width), BF)
    far_send, near_send, nbr, cnt = call(
        head_kernel,
        "head",
        (features, neighbours.T, counts.reshape(2, half)),
        [rim_t, rim_t, ((slots, atoms), jnp.int32), ((2, half), jnp.int32)],
        4,
        scratch=[dma((4,))],
        in_specs=[HB] * 3,
        flops=10**12,
    )
    far = lax.ppermute(far_send, "cell", wrapped)
    near = lax.ppermute(near_send, "cell", inside)
    pick, total, gate, dgate, selfs = call(
        functools.partial(front_kernel, slots=slots),
        "front",
        (
            nbr, cnt, features,
            radial.reshape(atoms * slots, basis), cotangent.reshape(atoms * slots, entries),
            w_self, w_neighbour, w_radial, w_block,
        ),
        [((2 * edges, 4 * half), BF), both_t, both_t, both_t, grad_t],
        16,
    )
    refs = (selfs, total, gate, dgate, pick)
    side_t = [edge_t, edge_t, rim_t]
    near_msg, near_adj, near_rim = call(near_kernel, "near", (near, w_neighbour) + refs, side_t, 12)
    far_msg, far_adj, far_rim = call(
        far_kernel, "far", (far, w_neighbour) + refs + (near_rim,), side_t, 12
    )
    near_rim, far_rim = lax.optimization_barrier((near_rim, far_rim))
    near_back = lax.ppermute(near_rim, "cell", inside)
    far_back = lax.ppermute(far_rim, "cell", across)
    blocks, grad = call(
        own_kernel,
        "own",
        (near_msg, far_msg, near_adj, far_adj, pick, w_self, w_neighbour, w_block),
        [((2 * edges, entries), BF), ((atoms, width), F32)],
        16,
        scratch=[
            pltpu.VMEM((edges, entries), BF),
            pltpu.VMEM((edges, entries), BF),
            pltpu.VMEM((atoms, width), BF),
            dma((2,)),
        ],
        out_specs=[HB, VM],
    )
    (feat_grad,) = call(
        last_kernel,
        "last",
        (far_back, near_back, grad, w_neighbour),
        [grad_t],
        4,
        scratch=[pltpu.VMEM((half, width), BF), pltpu.VMEM((half, width), BF), dma((2,))],
        out_specs=[HB],
    )
    return blocks.reshape(atoms, slots, entries), feat_grad


def solution(mesh):
    in_specs = (
        P("cell", None),
        P("cell", None, None),
        P("cell", None),
        P("cell"),
        P("cell", None, None),
        P(),
        P(),
        P(),
        P(),
    )
    out_specs = (P("cell", None, None), P("cell", None))
    return jax.shard_map(
        functools.partial(body, mesh.shape["cell"]),
        mesh=mesh, in_specs=in_specs, out_specs=out_specs, check_vma=False,
    )
```

```python
import functools

import jax
import jax.numpy as jnp
from jax import lax
from jax.experimental import pallas as pl
from jax.experimental.pallas import tpu as pltpu
from jax.sharding import PartitionSpec as P

BF = jnp.bfloat16
F32 = jnp.float32


def mm(a, b):
    return jnp.dot(a, b, preferred_element_type=F32)


def mm_nt(a, b):
    return lax.dot_general(a, b, (((1,), (1,)), ((), ())), preferred_element_type=F32)


def mm_tn(a, b):
    return lax.dot_general(a, b, (((0,), (0,)), ((), ())), preferred_element_type=F32)


def halves(half):
    parity = lax.rem(lax.axis_index("cell"), 2)
    near, far = 1 - parity, parity
    return near, far, pl.multiple_of(near * half, half), pl.multiple_of(far * half, half)


def picker(nbr, count_row, base, half, slots):
    local = nbr - base
    own = (local >= 0) & (local < 2 * half)
    target = jnp.where(own, local, 2 * half + (local & (half - 1)))
    live = lax.broadcasted_iota(jnp.int32, (slots, half), 0) < count_row
    target = jnp.where(live, (target - half).astype(F32), -2.0 * half).astype(BF)
    edges = half * slots
    row = lax.broadcasted_iota(jnp.int32, (edges, half), 0)
    lane = lax.broadcasted_iota(jnp.int32, (edges, half), 1)
    one, zero = jnp.ones((), BF), jnp.zeros((), BF)
    lane_b = lane.astype(F32).astype(BF)
    same_atom = jnp.where(lane_b == (row // slots).astype(F32).astype(BF), one, zero)
    spread = mm_nt(same_atom, target)
    slot_lane = lax.broadcasted_iota(jnp.int32, (edges, slots), 1)
    slot_row = lax.broadcasted_iota(jnp.int32, (edges, slots), 0)
    mine = jnp.where((slot_row & (slots - 1)) == slot_lane, spread, 0.0)
    target = jnp.sum(mine, axis=1, keepdims=True)
    target = jnp.broadcast_to(target, (edges, half)).astype(BF)
    low, high, halo = [
        jnp.where(target == lane_b + BF(half * (j - 1)), one, zero) for j in range(3)
    ]
    mine = jnp.where(target > BF(-1.5 * half), same_atom, zero)
    return jnp.concatenate([low, high, mine, halo], axis=1)


def activation(total, half_gate, half_dgate):
    h = total * half_gate
    t = jnp.tanh(h)
    ht = h * t
    return h + ht, half_dgate * (t + BF(1.0)) * (h - ht + BF(1.0))


def head_kernel(feat_hbm, nbr_hbm, cnt_hbm, far_ref, near_ref, nbr_ref, cnt_ref, sems):
    half = far_ref.shape[0]
    _, _, near_off, far_off = halves(half)
    pairs = [
        (feat_hbm.at[pl.ds(far_off, half)], far_ref),
        (feat_hbm.at[pl.ds(near_off, half)], near_ref),
        (nbr_hbm, nbr_ref),
        (cnt_hbm, cnt_ref),
    ]
    copies = [pltpu.make_async_copy(src, dst, sems.at[n]) for n, (src, dst) in enumerate(pairs)]
    for copy in copies:
        copy.start()
    for copy in copies:
        copy.wait()


def prepare(half_index, own, refs, outs, slots):
    nbr_ref, cnt_ref, rad_ref, cot_ref, wrad_ref, wblk_ref = refs
    pick_ref, sum_ref, gate_ref, dgate_ref = outs
    edges = pick_ref.shape[0]
    half = edges // slots
    off = pl.multiple_of(half_index * half, half)
    rows = pl.ds(pl.multiple_of(half_index * edges, edges), edges)
    pick_ref[...] = picker(
        nbr_ref[:, pl.ds(off, half)],
        cnt_ref[pl.ds(half_index, 1), :],
        lax.axis_index("cell") * (2 * half),
        half,
        slots,
    )
    gate = mm(rad_ref[rows, :], wrad_ref[...] * BF(0.5))
    gate_ref[...] = gate.astype(BF)
    sum_ref[...] = mm(pick_ref[:, : 2 * half], own).astype(BF)
    dgate_ref[...] = (mm_nt(cot_ref[rows, :], wblk_ref[...]) * gate).astype(BF)


def front_kernel(
    nbr_ref, cnt_ref, rad_ref, cot_ref, wrad_ref, wblk_ref, feat_ref, wself_ref, wnbr_ref,
    pick_ref, sum_ref, gate_ref, dgate_ref, self_ref, own_ref,
    *, slots,
):
    _, far, _, _ = halves(feat_ref.shape[0] // 2)
    own = mm(feat_ref[...], wnbr_ref[...]).astype(BF)
    own_ref[...] = own
    self_ref[...] = mm(feat_ref[...], wself_ref[...]).astype(BF)
    refs = (nbr_ref, cnt_ref, rad_ref, cot_ref, wrad_ref, wblk_ref)
    prepare(far, own, refs, (pick_ref, sum_ref, gate_ref, dgate_ref), slots)


def side(halo, half_index, refs, msg_ref, adj_ref, rim_ref):
    self_ref, sum_ref, gate_ref, dgate_ref, pick_ref = refs
    half = rim_ref.shape[0]
    edges = msg_ref.shape[0]
    table = jnp.concatenate(
        [self_ref[pl.ds(pl.multiple_of(half_index * half, half), half), :], halo], axis=0
    )
    step = edges // 2
    chunks = [slice(n * step, (n + 1) * step) for n in range(2)]
    parts = [mm(pick_ref[rows, 2 * half :], table).astype(BF) for rows in chunks]
    for rows, part in zip(chunks, parts):
        message, adj = activation(sum_ref[rows, :] + part, gate_ref[rows, :], dgate_ref[rows, :])
        msg_ref[rows, :] = message
        adj_ref[rows, :] = adj
    rim_ref[...] = mm_tn(pick_ref[:, 3 * half :], adj_ref[...]).astype(BF)


def near_kernel(
    nbr_ref, cnt_ref, rad_ref, cot_ref, wrad_ref, wblk_ref, near_ref, wnbr_ref, self_ref, own_ref, order_ref,
    msg_ref, adj_ref, rim_ref, pick_ref,
    sum_ref, gate_ref, dgate_ref,
    *, slots,
):
    near, _, _, _ = halves(rim_ref.shape[0])
    refs = (nbr_ref, cnt_ref, rad_ref, cot_ref, wrad_ref, wblk_ref)
    prepare(near, own_ref[...], refs, (pick_ref, sum_ref, gate_ref, dgate_ref), slots)
    halo = mm(near_ref[...], wnbr_ref[...]).astype(BF)
    side(halo, near, (self_ref, sum_ref, gate_ref, dgate_ref, pick_ref), msg_ref, adj_ref, rim_ref)


def far_kernel(
    far_ref, wnbr_ref, self_ref, sum_ref, gate_ref, dgate_ref, pick_ref, msg_ref, adj_ref, rim_ref
):
    _, far, _, _ = halves(rim_ref.shape[0])
    halo = mm(far_ref[...], wnbr_ref[...]).astype(BF)
    side(halo, far, (self_ref, sum_ref, gate_ref, dgate_ref, pick_ref), msg_ref, adj_ref, rim_ref)


def own_kernel(
    nearmsg_ref, farmsg_ref, nearadj_ref, faradj_ref, nearpick_ref, farpick_ref, wself_ref, wnbr_ref, wblk_ref,
    blocks_hbm, grad_ref,
    nearblk_ref, farblk_ref, selfsum_ref, sems,
):
    edges = farmsg_ref.shape[0]
    atoms = grad_ref.shape[0]
    half = atoms // 2
    near, far, near_off, far_off = halves(half)
    near_edge = pl.multiple_of(near * edges, edges)
    far_edge = pl.multiple_of(far * edges, edges)
    farblk_ref[...] = mm(farmsg_ref[...], wblk_ref[...]).astype(BF)
    far_copy = pltpu.make_async_copy(farblk_ref, blocks_hbm.at[pl.ds(far_edge, edges)], sems.at[0])
    far_copy.start()
    nearblk_ref[...] = mm(nearmsg_ref[...], wblk_ref[...]).astype(BF)
    near_copy = pltpu.make_async_copy(
        nearblk_ref, blocks_hbm.at[pl.ds(near_edge, edges)], sems.at[1]
    )
    near_copy.start()

    @pl.when(lax.axis_index("cell") >= 0)
    def _():
        near_back = mm_tn(nearpick_ref[:, : atoms + half], nearadj_ref[...])
        far_back = mm_tn(farpick_ref[:, : atoms + half], faradj_ref[...])
        selfsum_ref[pl.ds(near_off, half), :] = near_back[atoms:].astype(BF)
        selfsum_ref[pl.ds(far_off, half), :] = far_back[atoms:].astype(BF)
        total = (near_back[:atoms] + far_back[:atoms]).astype(BF)
        grad_ref[...] = mm_nt(total, wnbr_ref[...]) + mm_nt(selfsum_ref[...], wself_ref[...])

    near_copy.wait()
    far_copy.wait()


def last_kernel(far_ref, near_ref, grad_ref, wnbr_ref, out_hbm, fout_ref, nout_ref, sem):
    half = near_ref.shape[0]
    _, _, near_off, far_off = halves(half)
    fout_ref[...] = (grad_ref[pl.ds(far_off, half), :] + mm_nt(far_ref[...], wnbr_ref[...])).astype(BF)
    c0 = pltpu.make_async_copy(fout_ref, out_hbm.at[pl.ds(far_off, half)], sem.at[0])
    c0.start()
    nout_ref[...] = (grad_ref[pl.ds(near_off, half), :] + mm_nt(near_ref[...], wnbr_ref[...])).astype(BF)
    c1 = pltpu.make_async_copy(nout_ref, out_hbm.at[pl.ds(near_off, half)], sem.at[1])
    c1.start()
    c0.wait()
    c1.wait()


VM = pl.BlockSpec(memory_space=pltpu.VMEM)
HB = pl.BlockSpec(memory_space=pltpu.HBM)


def call(kernel, name, inputs, outs, megabytes, scratch=(), in_specs=None, out_specs=None, flops=0):
    in_specs = in_specs or [VM] * len(inputs)
    inputs = [
        pltpu.with_memory_space_constraint(x, pltpu.HBM) if spec is HB else x
        for x, spec in zip(inputs, in_specs)
    ]
    return pl.pallas_call(
        kernel,
        name=name,
        out_shape=[jax.ShapeDtypeStruct(shape, dtype) for shape, dtype in outs],
        in_specs=in_specs,
        out_specs=out_specs or [VM] * len(outs),
        scratch_shapes=list(scratch),
        cost_estimate=pl.CostEstimate(flops=flops, bytes_accessed=0, transcendentals=0),
        compiler_params=pltpu.CompilerParams(vmem_limit_bytes=megabytes * 1024 * 1024),
    )(*inputs)


def body(count, features, radial, neighbours, counts, cotangent, w_self, w_neighbour, w_radial, w_block):
    atoms, width = features.shape
    slots = neighbours.shape[1]
    half = atoms // 2
    edges = half * slots
    entries = w_block.shape[1]
    basis = radial.shape[2]
    inside = [(i, i ^ 1) for i in range(count)]
    across = []
    for i in range(1, count - 1, 2):
        across += [(i, i + 1), (i + 1, i)]
    wrapped = across + [(0, count - 1), (count - 1, 0)]
    dma = pltpu.SemaphoreType.DMA
    edge_t = ((edges, width), BF)
    rim_t = ((half, width), BF)
    grad_t = ((atoms, width), BF)
    far_send, near_send, nbr, cnt = call(
        head_kernel,
        "head",
        (features, neighbours.T, counts.reshape(2, half)),
        [rim_t, rim_t, ((slots, atoms), jnp.int32), ((2, half), jnp.int32)],
        4,
        scratch=[dma((4,))],
        in_specs=[HB] * 3,
        flops=10**12,
    )
    far = lax.ppermute(far_send, "cell", across)
    near = lax.ppermute(near_send, "cell", inside)
    pick_t = ((edges, 4 * half), BF)
    edge_refs = (
        nbr, cnt, radial.reshape(atoms * slots, basis), cotangent.reshape(atoms * slots, entries),
        w_radial, w_block,
    )
    far_pick, total, gate, dgate, selfs, own = call(
        functools.partial(front_kernel, slots=slots),
        "front",
        edge_refs + (features, w_self, w_neighbour),
        [pick_t, edge_t, edge_t, edge_t, grad_t, grad_t],
        16,
    )
    side_t = [edge_t, edge_t, rim_t]
    far_msg, far_adj, far_rim = call(
        far_kernel, "far", (far, w_neighbour, selfs, total, gate, dgate, far_pick), side_t, 12
    )
    far_back = lax.ppermute(far_rim, "cell", wrapped)
    near_msg, near_adj, near_rim, near_pick = call(
        functools.partial(near_kernel, slots=slots),
        "near",
        edge_refs + (near, w_neighbour, selfs, own, far_msg),
        side_t + [pick_t],
        16,
        scratch=[pltpu.VMEM((edges, width), BF)] * 3,
    )
    near_back = lax.ppermute(near_rim, "cell", inside)
    blocks, grad = call(
        own_kernel,
        "own",
        (near_msg, far_msg, near_adj, far_adj, near_pick, far_pick, w_self, w_neighbour, w_block),
        [((2 * edges, entries), BF), ((atoms, width), F32)],
        16,
        scratch=[
            pltpu.VMEM((edges, entries), BF),
            pltpu.VMEM((edges, entries), BF),
            pltpu.VMEM((atoms, width), BF),
            dma((2,)),
        ],
        out_specs=[HB, VM],
    )
    (feat_grad,) = call(
        last_kernel,
        "last",
        (far_back, near_back, grad, w_neighbour),
        [grad_t],
        4,
        scratch=[pltpu.VMEM((half, width), BF), pltpu.VMEM((half, width), BF), dma((2,))],
        out_specs=[HB],
    )
    return blocks.reshape(atoms, slots, entries), feat_grad


def solution(mesh):
    in_specs = (
        P("cell", None),
        P("cell", None, None),
        P("cell", None),
        P("cell"),
        P("cell", None, None),
        P(),
        P(),
        P(),
        P(),
    )
    out_specs = (P("cell", None, None), P("cell", None))
    return jax.shard_map(
        functools.partial(body, mesh.shape["cell"]),
        mesh=mesh, in_specs=in_specs, out_specs=out_specs, check_vma=False,
    )
```

```python
import functools

import jax
import jax.numpy as jnp
from jax import lax
from jax.experimental import pallas as pl
from jax.experimental.pallas import tpu as pltpu
from jax.sharding import PartitionSpec as P

BF = jnp.bfloat16
F32 = jnp.float32


def mm(a, b):
    return jnp.dot(a, b, preferred_element_type=F32)


def mm_nt(a, b):
    return lax.dot_general(a, b, (((1,), (1,)), ((), ())), preferred_element_type=F32)


def mm_tn(a, b):
    return lax.dot_general(a, b, (((0,), (0,)), ((), ())), preferred_element_type=F32)


def swaps(pairs):
    return [edge for a, b in pairs for edge in ((a, b), (b, a))]


def in_first(device):
    return ((device + 1) // 2 + 1) // 4 % 2 == 0


def chip_swaps(count):
    across = [(i, i + 1) for i in range(1, count - 1, 2)]
    if count < 16 or count % 8:
        return swaps(across), swaps(across)
    both = []
    for first in (True, False):
        pairs = [pair for pair in across if in_first(pair[0]) == first]
        busy = {device for pair in pairs for device in pair}
        rest = [device for device in range(count) if device not in busy]
        both.append(swaps(pairs + list(zip(rest[::2], rest[1::2]))))
    return both


def from_across(count, first_ref, second_ref):
    device = lax.axis_index("cell")
    value = jnp.where(in_first(device), first_ref[...], second_ref[...])
    inner = (device > 0) & (device < count - 1)
    return jnp.where(inner, value, jnp.zeros_like(value))


def halves(half):
    parity = lax.rem(lax.axis_index("cell"), 2)
    near, far = 1 - parity, parity
    return near, far, pl.multiple_of(near * half, half), pl.multiple_of(far * half, half)


def picker(nbr, count_row, base, half, slots):
    local = nbr - base
    own = (local >= 0) & (local < 2 * half)
    target = jnp.where(own, local, 2 * half + (local & (half - 1)))
    live = lax.broadcasted_iota(jnp.int32, (slots, half), 0) < count_row
    target = jnp.where(live, (target - half).astype(F32), -2.0 * half).astype(BF)
    edges = half * slots
    row = lax.broadcasted_iota(jnp.int32, (edges, half), 0)
    lane = lax.broadcasted_iota(jnp.int32, (edges, half), 1)
    one, zero = jnp.ones((), BF), jnp.zeros((), BF)
    lane_b = lane.astype(F32).astype(BF)
    same_atom = jnp.where(lane_b == (row // slots).astype(F32).astype(BF), one, zero)
    spread = mm_nt(same_atom, target)
    slot_lane = lax.broadcasted_iota(jnp.int32, (edges, slots), 1)
    slot_row = lax.broadcasted_iota(jnp.int32, (edges, slots), 0)
    mine = jnp.where((slot_row & (slots - 1)) == slot_lane, spread, 0.0)
    target = jnp.sum(mine, axis=1, keepdims=True)
    target = jnp.broadcast_to(target, (edges, half)).astype(BF)
    low, high, halo = [
        jnp.where(target == lane_b + BF(half * (j - 1)), one, zero) for j in range(3)
    ]
    mine = jnp.where(target > BF(-1.5 * half), same_atom, zero)
    return jnp.concatenate([low, high, mine, halo], axis=1)


def activation(total, half_gate, half_dgate):
    h = total * half_gate
    t = jnp.tanh(h)
    ht = h * t
    return h + ht, half_dgate * (t + BF(1.0)) * (h - ht + BF(1.0))


def head_kernel(feat_hbm, nbr_hbm, cnt_hbm, far_ref, near_ref, nbr_ref, cnt_ref, sems):
    half = far_ref.shape[0]
    _, _, near_off, far_off = halves(half)
    pairs = [
        (feat_hbm.at[pl.ds(far_off, half)], far_ref),
        (feat_hbm.at[pl.ds(near_off, half)], near_ref),
        (nbr_hbm, nbr_ref),
        (cnt_hbm, cnt_ref),
    ]
    copies = [pltpu.make_async_copy(src, dst, sems.at[n]) for n, (src, dst) in enumerate(pairs)]
    for copy in copies:
        copy.start()
    for copy in copies:
        copy.wait()


def prepare(half_index, own, refs, outs, slots):
    nbr_ref, cnt_ref, rad_ref, cot_ref, wrad_ref, wblk_ref = refs
    pick_ref, sum_ref, gate_ref, dgate_ref = outs
    edges = pick_ref.shape[0]
    half = edges // slots
    off = pl.multiple_of(half_index * half, half)
    rows = pl.ds(pl.multiple_of(half_index * edges, edges), edges)
    pick_ref[...] = picker(
        nbr_ref[:, pl.ds(off, half)],
        cnt_ref[pl.ds(half_index, 1), :],
        lax.axis_index("cell") * (2 * half),
        half,
        slots,
    )
    gate = mm(rad_ref[rows, :], wrad_ref[...] * BF(0.5))
    gate_ref[...] = gate.astype(BF)
    sum_ref[...] = mm(pick_ref[:, : 2 * half], own).astype(BF)
    dgate_ref[...] = (mm_nt(cot_ref[rows, :], wblk_ref[...]) * gate).astype(BF)


def front_kernel(
    nbr_ref, cnt_ref, rad_ref, cot_ref, wrad_ref, wblk_ref, feat_ref, wself_ref, wnbr_ref,
    pick_ref, sum_ref, gate_ref, dgate_ref, self_ref, own_ref,
    *, slots,
):
    _, far, _, _ = halves(feat_ref.shape[0] // 2)
    own = mm(feat_ref[...], wnbr_ref[...]).astype(BF)
    own_ref[...] = own
    self_ref[...] = mm(feat_ref[...], wself_ref[...]).astype(BF)
    refs = (nbr_ref, cnt_ref, rad_ref, cot_ref, wrad_ref, wblk_ref)
    prepare(far, own, refs, (pick_ref, sum_ref, gate_ref, dgate_ref), slots)


def side(halo, half_index, refs, msg_ref, adj_ref, rim_ref):
    self_ref, sum_ref, gate_ref, dgate_ref, pick_ref = refs
    half = rim_ref.shape[0]
    edges = msg_ref.shape[0]
    table = jnp.concatenate(
        [self_ref[pl.ds(pl.multiple_of(half_index * half, half), half), :], halo], axis=0
    )
    step = edges // 2
    chunks = [slice(n * step, (n + 1) * step) for n in range(2)]
    parts = [mm(pick_ref[rows, 2 * half :], table).astype(BF) for rows in chunks]
    for rows, part in zip(chunks, parts):
        message, adj = activation(sum_ref[rows, :] + part, gate_ref[rows, :], dgate_ref[rows, :])
        msg_ref[rows, :] = message
        adj_ref[rows, :] = adj
    rim_ref[...] = mm_tn(pick_ref[:, 3 * half :], adj_ref[...]).astype(BF)


def near_kernel(
    nbr_ref, cnt_ref, rad_ref, cot_ref, wrad_ref, wblk_ref, near_ref, wnbr_ref, self_ref, own_ref,
    msg_ref, adj_ref, rim_ref, pick_ref,
    sum_ref, gate_ref, dgate_ref,
    *, slots,
):
    near, _, _, _ = halves(rim_ref.shape[0])
    refs = (nbr_ref, cnt_ref, rad_ref, cot_ref, wrad_ref, wblk_ref)
    prepare(near, own_ref[...], refs, (pick_ref, sum_ref, gate_ref, dgate_ref), slots)
    halo = mm(near_ref[...], wnbr_ref[...]).astype(BF)
    side(halo, near, (self_ref, sum_ref, gate_ref, dgate_ref, pick_ref), msg_ref, adj_ref, rim_ref)


def far_kernel(
    second_ref, first_ref, wnbr_ref, self_ref, sum_ref, gate_ref, dgate_ref, pick_ref, order_ref,
    msg_ref, adj_ref, rim_ref,
    *, count,
):
    _, far, _, _ = halves(rim_ref.shape[0])
    halo = mm(from_across(count, first_ref, second_ref), wnbr_ref[...]).astype(BF)
    side(halo, far, (self_ref, sum_ref, gate_ref, dgate_ref, pick_ref), msg_ref, adj_ref, rim_ref)


def own_kernel(
    nearmsg_ref, farmsg_ref, nearadj_ref, faradj_ref, nearpick_ref, farpick_ref, wself_ref, wnbr_ref, wblk_ref,
    blocks_hbm, grad_ref,
    nearblk_ref, farblk_ref, selfsum_ref, sems,
):
    edges = farmsg_ref.shape[0]
    atoms = grad_ref.shape[0]
    half = atoms // 2
    near, far, near_off, far_off = halves(half)
    near_edge = pl.multiple_of(near * edges, edges)
    far_edge = pl.multiple_of(far * edges, edges)
    farblk_ref[...] = mm(farmsg_ref[...], wblk_ref[...]).astype(BF)
    far_copy = pltpu.make_async_copy(farblk_ref, blocks_hbm.at[pl.ds(far_edge, edges)], sems.at[0])
    far_copy.start()
    nearblk_ref[...] = mm(nearmsg_ref[...], wblk_ref[...]).astype(BF)
    near_copy = pltpu.make_async_copy(
        nearblk_ref, blocks_hbm.at[pl.ds(near_edge, edges)], sems.at[1]
    )
    near_copy.start()

    @pl.when(lax.axis_index("cell") >= 0)
    def _():
        near_back = mm_tn(nearpick_ref[:, : atoms + half], nearadj_ref[...])
        far_back = mm_tn(farpick_ref[:, : atoms + half], faradj_ref[...])
        selfsum_ref[pl.ds(near_off, half), :] = near_back[atoms:].astype(BF)
        selfsum_ref[pl.ds(far_off, half), :] = far_back[atoms:].astype(BF)
        total = (near_back[:atoms] + far_back[:atoms]).astype(BF)
        grad_ref[...] = mm_nt(total, wnbr_ref[...]) + mm_nt(selfsum_ref[...], wself_ref[...])

    near_copy.wait()
    far_copy.wait()


def last_kernel(second_ref, first_ref, near_ref, grad_ref, wnbr_ref, out_hbm, out_ref, sem, *, count):
    half = near_ref.shape[0]
    _, _, near_off, far_off = halves(half)
    rims = jnp.concatenate([from_across(count, first_ref, second_ref), near_ref[...]], axis=0)
    grads = jnp.concatenate(
        [grad_ref[pl.ds(far_off, half), :], grad_ref[pl.ds(near_off, half), :]], axis=0
    )
    total = (grads + mm_nt(rims, wnbr_ref[...])).astype(BF)
    out_ref[pl.ds(far_off, half), :] = total[:half]
    out_ref[pl.ds(near_off, half), :] = total[half:]
    copy = pltpu.make_async_copy(out_ref, out_hbm, sem)
    copy.start()
    copy.wait()


VM = pl.BlockSpec(memory_space=pltpu.VMEM)
HB = pl.BlockSpec(memory_space=pltpu.HBM)


def call(kernel, name, inputs, outs, megabytes, scratch=(), in_specs=None, out_specs=None, flops=0):
    in_specs = in_specs or [VM] * len(inputs)
    inputs = [
        pltpu.with_memory_space_constraint(x, pltpu.HBM) if spec is HB else x
        for x, spec in zip(inputs, in_specs)
    ]
    return pl.pallas_call(
        kernel,
        name=name,
        out_shape=[jax.ShapeDtypeStruct(shape, dtype) for shape, dtype in outs],
        in_specs=in_specs,
        out_specs=out_specs or [VM] * len(outs),
        scratch_shapes=list(scratch),
        cost_estimate=pl.CostEstimate(flops=flops, bytes_accessed=0, transcendentals=0),
        compiler_params=pltpu.CompilerParams(vmem_limit_bytes=megabytes * 1024 * 1024),
    )(*inputs)


def body(count, features, radial, neighbours, counts, cotangent, w_self, w_neighbour, w_radial, w_block):
    atoms, width = features.shape
    slots = neighbours.shape[1]
    half = atoms // 2
    edges = half * slots
    entries = w_block.shape[1]
    basis = radial.shape[2]
    inside = [(i, i ^ 1) for i in range(count)]
    first, second = chip_swaps(count)
    dma = pltpu.SemaphoreType.DMA
    edge_t = ((edges, width), BF)
    rim_t = ((half, width), BF)
    grad_t = ((atoms, width), BF)
    far_send, near_send, nbr, cnt = call(
        head_kernel,
        "head",
        (features, neighbours.T, counts.reshape(2, half)),
        [rim_t, rim_t, ((slots, atoms), jnp.int32), ((2, half), jnp.int32)],
        4,
        scratch=[dma((4,))],
        in_specs=[HB] * 3,
        flops=10**12,
    )
    far_first = lax.ppermute(far_send, "cell", first)
    far_second = lax.ppermute(far_send, "cell", second)
    near = lax.ppermute(near_send, "cell", inside)
    pick_t = ((edges, 4 * half), BF)
    edge_refs = (
        nbr, cnt, radial.reshape(atoms * slots, basis), cotangent.reshape(atoms * slots, entries),
        w_radial, w_block,
    )
    far_pick, total, gate, dgate, selfs, own = call(
        functools.partial(front_kernel, slots=slots),
        "front",
        edge_refs + (features, w_self, w_neighbour),
        [pick_t, edge_t, edge_t, edge_t, grad_t, grad_t],
        16,
    )
    side_t = [edge_t, edge_t, rim_t]
    near_msg, near_adj, near_rim, near_pick = call(
        functools.partial(near_kernel, slots=slots),
        "near",
        edge_refs + (near, w_neighbour, selfs, own),
        side_t + [pick_t],
        16,
        scratch=[pltpu.VMEM((edges, width), BF)] * 3,
    )
    near_back = lax.ppermute(near_rim, "cell", inside)
    far_msg, far_adj, far_rim = call(
        functools.partial(far_kernel, count=count),
        "far",
        (far_second, far_first, w_neighbour, selfs, total, gate, dgate, far_pick, near_msg),
        side_t,
        12,
    )
    far_back_second = lax.ppermute(far_rim, "cell", second)
    far_back_first = lax.ppermute(far_rim, "cell", first)
    blocks, grad = call(
        own_kernel,
        "own",
        (near_msg, far_msg, near_adj, far_adj, near_pick, far_pick, w_self, w_neighbour, w_block),
        [((2 * edges, entries), BF), ((atoms, width), F32)],
        16,
        scratch=[
            pltpu.VMEM((edges, entries), BF),
            pltpu.VMEM((edges, entries), BF),
            pltpu.VMEM((atoms, width), BF),
            dma((2,)),
        ],
        out_specs=[HB, VM],
    )
    (feat_grad,) = call(
        functools.partial(last_kernel, count=count),
        "last",
        (far_back_second, far_back_first, near_back, grad, w_neighbour),
        [grad_t],
        4,
        scratch=[pltpu.VMEM((atoms, width), BF), dma],
        out_specs=[HB],
    )
    return blocks.reshape(atoms, slots, entries), feat_grad


def solution(mesh):
    in_specs = (
        P("cell", None),
        P("cell", None, None),
        P("cell", None),
        P("cell"),
        P("cell", None, None),
        P(),
        P(),
        P(),
        P(),
    )
    out_specs = (P("cell", None, None), P("cell", None))
    return jax.shard_map(
        functools.partial(body, mesh.shape["cell"]),
        mesh=mesh, in_specs=in_specs, out_specs=out_specs, check_vma=False,
    )
```

```python
import functools

import jax
import jax.numpy as jnp
from jax import lax
from jax.experimental import pallas as pl
from jax.experimental.pallas import tpu as pltpu
from jax.sharding import PartitionSpec as P

BF = jnp.bfloat16
F32 = jnp.float32


def mm(a, b):
    return jnp.dot(a, b, preferred_element_type=F32)


def mm_nt(a, b):
    return lax.dot_general(a, b, (((1,), (1,)), ((), ())), preferred_element_type=F32)


def mm_tn(a, b):
    return lax.dot_general(a, b, (((0,), (0,)), ((), ())), preferred_element_type=F32)


def swaps(pairs):
    return [edge for a, b in pairs for edge in ((a, b), (b, a))]


def in_first(device):
    return ((device + 1) // 2 + 1) // 4 % 2 == 0


def chip_swaps(count):
    across = [(i, i + 1) for i in range(1, count - 1, 2)]
    if count < 16 or count % 8:
        return swaps(across), swaps(across)
    both = []
    for first in (True, False):
        pairs = [pair for pair in across if in_first(pair[0]) == first]
        busy = {device for pair in pairs for device in pair}
        rest = [device for device in range(count) if device not in busy]
        both.append(swaps(pairs + list(zip(rest[::2], rest[1::2]))))
    return both


def from_across(count, first_ref, second_ref):
    device = lax.axis_index("cell")
    value = jnp.where(in_first(device), first_ref[...], second_ref[...])
    inner = (device > 0) & (device < count - 1)
    return jnp.where(inner, value, jnp.zeros_like(value))


def halves(half):
    parity = lax.rem(lax.axis_index("cell"), 2)
    near, far = 1 - parity, parity
    return near, far, pl.multiple_of(near * half, half), pl.multiple_of(far * half, half)


def picker(nbr, count_row, base, half, slots):
    local = nbr - base
    own = (local >= 0) & (local < 2 * half)
    target = jnp.where(own, local, 2 * half + (local & (half - 1)))
    live = lax.broadcasted_iota(jnp.int32, (slots, half), 0) < count_row
    target = jnp.where(live, (target - half).astype(F32), -2.0 * half).astype(BF)
    edges = half * slots
    row = lax.broadcasted_iota(jnp.int32, (edges, half), 0)
    lane = lax.broadcasted_iota(jnp.int32, (edges, half), 1)
    one, zero = jnp.ones((), BF), jnp.zeros((), BF)
    lane_b = lane.astype(F32).astype(BF)
    same_atom = jnp.where(lane_b == (row // slots).astype(F32).astype(BF), one, zero)
    spread = mm_nt(same_atom, target)
    slot_lane = lax.broadcasted_iota(jnp.int32, (edges, slots), 1)
    slot_row = lax.broadcasted_iota(jnp.int32, (edges, slots), 0)
    mine = jnp.where((slot_row & (slots - 1)) == slot_lane, spread, 0.0)
    target = jnp.sum(mine, axis=1, keepdims=True)
    target = jnp.broadcast_to(target, (edges, half)).astype(BF)
    low, high, halo = [
        jnp.where(target == lane_b + BF(half * (j - 1)), one, zero) for j in range(3)
    ]
    mine = jnp.where(target > BF(-1.5 * half), same_atom, zero)
    return jnp.concatenate([low, high, mine, halo], axis=1)


def activation(total, gate, dgate):
    v = total * gate
    e = jnp.exp(jnp.minimum(-v, BF(80.0)))
    s = pl.reciprocal(e + BF(1.0), approx=True)
    message = v * s
    return message, dgate * s * (message * e + BF(1.0))


def head_kernel(feat_hbm, nbr_hbm, cnt_hbm, far_ref, near_ref, nbr_ref, cnt_ref, sems):
    half = far_ref.shape[0]
    _, _, near_off, far_off = halves(half)
    pairs = [
        (feat_hbm.at[pl.ds(far_off, half)], far_ref),
        (feat_hbm.at[pl.ds(near_off, half)], near_ref),
        (nbr_hbm, nbr_ref),
        (cnt_hbm, cnt_ref),
    ]
    copies = [pltpu.make_async_copy(src, dst, sems.at[n]) for n, (src, dst) in enumerate(pairs)]
    for copy in copies:
        copy.start()
    for copy in copies:
        copy.wait()


def prepare(half_index, own, refs, outs, slots):
    nbr_ref, cnt_ref, rad_ref, cot_ref, wrad_ref, wblk_ref = refs
    pick_ref, sum_ref, gate_ref, dgate_ref = outs
    edges = pick_ref.shape[0]
    half = edges // slots
    off = pl.multiple_of(half_index * half, half)
    rows = pl.ds(pl.multiple_of(half_index * edges, edges), edges)
    pick_ref[...] = picker(
        nbr_ref[:, pl.ds(off, half)],
        cnt_ref[pl.ds(half_index, 1), :],
        lax.axis_index("cell") * (2 * half),
        half,
        slots,
    )
    gate = mm(rad_ref[rows, :], wrad_ref[...])
    gate_ref[...] = gate.astype(BF)
    sum_ref[...] = mm(pick_ref[:, : 2 * half], own).astype(BF)
    dgate_ref[...] = (mm_nt(cot_ref[rows, :], wblk_ref[...]) * gate).astype(BF)


def front_kernel(
    nbr_ref, cnt_ref, rad_ref, cot_ref, wrad_ref, wblk_ref, feat_ref, wself_ref, wnbr_ref,
    pick_ref, sum_ref, gate_ref, dgate_ref, self_ref, own_ref,
    *, slots,
):
    _, far, _, _ = halves(feat_ref.shape[0] // 2)
    own = mm(feat_ref[...], wnbr_ref[...]).astype(BF)
    own_ref[...] = own
    self_ref[...] = mm(feat_ref[...], wself_ref[...]).astype(BF)
    refs = (nbr_ref, cnt_ref, rad_ref, cot_ref, wrad_ref, wblk_ref)
    prepare(far, own, refs, (pick_ref, sum_ref, gate_ref, dgate_ref), slots)


def side(halo, half_index, refs, msg_ref, adj_ref, rim_ref):
    self_ref, sum_ref, gate_ref, dgate_ref, pick_ref = refs
    half = rim_ref.shape[0]
    edges = msg_ref.shape[0]
    table = jnp.concatenate(
        [self_ref[pl.ds(pl.multiple_of(half_index * half, half), half), :], halo], axis=0
    )
    step = edges // 2
    chunks = [slice(n * step, (n + 1) * step) for n in range(2)]
    parts = [mm(pick_ref[rows, 2 * half :], table).astype(BF) for rows in chunks]
    for rows, part in zip(chunks, parts):
        message, adj = activation(sum_ref[rows, :] + part, gate_ref[rows, :], dgate_ref[rows, :])
        msg_ref[rows, :] = message
        adj_ref[rows, :] = adj
    rim_ref[...] = mm_tn(pick_ref[:, 3 * half :], adj_ref[...]).astype(BF)


def near_kernel(
    nbr_ref, cnt_ref, rad_ref, cot_ref, wrad_ref, wblk_ref, near_ref, wnbr_ref, self_ref, own_ref,
    msg_ref, adj_ref, rim_ref, pick_ref,
    sum_ref, gate_ref, dgate_ref,
    *, slots,
):
    near, _, _, _ = halves(rim_ref.shape[0])
    refs = (nbr_ref, cnt_ref, rad_ref, cot_ref, wrad_ref, wblk_ref)
    prepare(near, own_ref[...], refs, (pick_ref, sum_ref, gate_ref, dgate_ref), slots)
    halo = mm(near_ref[...], wnbr_ref[...]).astype(BF)
    side(halo, near, (self_ref, sum_ref, gate_ref, dgate_ref, pick_ref), msg_ref, adj_ref, rim_ref)


def far_kernel(
    second_ref, first_ref, wnbr_ref, self_ref, sum_ref, gate_ref, dgate_ref, pick_ref, order_ref,
    msg_ref, adj_ref, rim_ref,
    *, count,
):
    _, far, _, _ = halves(rim_ref.shape[0])
    halo = mm(from_across(count, first_ref, second_ref), wnbr_ref[...]).astype(BF)
    side(halo, far, (self_ref, sum_ref, gate_ref, dgate_ref, pick_ref), msg_ref, adj_ref, rim_ref)


def own_kernel(
    nearmsg_ref, farmsg_ref, nearadj_ref, faradj_ref, nearpick_ref, farpick_ref, wself_ref, wnbr_ref, wblk_ref,
    blocks_hbm, grad_ref,
    nearblk_ref, farblk_ref, selfsum_ref, sems,
):
    edges = farmsg_ref.shape[0]
    atoms = grad_ref.shape[0]
    half = atoms // 2
    near, far, near_off, far_off = halves(half)
    near_edge = pl.multiple_of(near * edges, edges)
    far_edge = pl.multiple_of(far * edges, edges)
    farblk_ref[...] = mm(farmsg_ref[...], wblk_ref[...]).astype(BF)
    far_copy = pltpu.make_async_copy(farblk_ref, blocks_hbm.at[pl.ds(far_edge, edges)], sems.at[0])
    far_copy.start()
    nearblk_ref[...] = mm(nearmsg_ref[...], wblk_ref[...]).astype(BF)
    near_copy = pltpu.make_async_copy(
        nearblk_ref, blocks_hbm.at[pl.ds(near_edge, edges)], sems.at[1]
    )
    near_copy.start()

    @pl.when(lax.axis_index("cell") >= 0)
    def _():
        near_back = mm_tn(nearpick_ref[:, : atoms + half], nearadj_ref[...])
        far_back = mm_tn(farpick_ref[:, : atoms + half], faradj_ref[...])
        selfsum_ref[pl.ds(near_off, half), :] = near_back[atoms:].astype(BF)
        selfsum_ref[pl.ds(far_off, half), :] = far_back[atoms:].astype(BF)
        total = (near_back[:atoms] + far_back[:atoms]).astype(BF)
        grad_ref[...] = mm_nt(total, wnbr_ref[...]) + mm_nt(selfsum_ref[...], wself_ref[...])

    near_copy.wait()
    far_copy.wait()


def last_kernel(second_ref, first_ref, near_ref, grad_ref, wnbr_ref, out_hbm, out_ref, sem, *, count):
    half = near_ref.shape[0]
    _, _, near_off, far_off = halves(half)
    rims = jnp.concatenate([from_across(count, first_ref, second_ref), near_ref[...]], axis=0)
    grads = jnp.concatenate(
        [grad_ref[pl.ds(far_off, half), :], grad_ref[pl.ds(near_off, half), :]], axis=0
    )
    total = (grads + mm_nt(rims, wnbr_ref[...])).astype(BF)
    out_ref[pl.ds(far_off, half), :] = total[:half]
    out_ref[pl.ds(near_off, half), :] = total[half:]
    copy = pltpu.make_async_copy(out_ref, out_hbm, sem)
    copy.start()
    copy.wait()


VM = pl.BlockSpec(memory_space=pltpu.VMEM)
HB = pl.BlockSpec(memory_space=pltpu.HBM)


def call(kernel, name, inputs, outs, megabytes, scratch=(), in_specs=None, out_specs=None, flops=0):
    in_specs = in_specs or [VM] * len(inputs)
    inputs = [
        pltpu.with_memory_space_constraint(x, pltpu.HBM) if spec is HB else x
        for x, spec in zip(inputs, in_specs)
    ]
    return pl.pallas_call(
        kernel,
        name=name,
        out_shape=[jax.ShapeDtypeStruct(shape, dtype) for shape, dtype in outs],
        in_specs=in_specs,
        out_specs=out_specs or [VM] * len(outs),
        scratch_shapes=list(scratch),
        cost_estimate=pl.CostEstimate(flops=flops, bytes_accessed=0, transcendentals=0),
        compiler_params=pltpu.CompilerParams(vmem_limit_bytes=megabytes * 1024 * 1024),
    )(*inputs)


def body(count, features, radial, neighbours, counts, cotangent, w_self, w_neighbour, w_radial, w_block):
    atoms, width = features.shape
    slots = neighbours.shape[1]
    half = atoms // 2
    edges = half * slots
    entries = w_block.shape[1]
    basis = radial.shape[2]
    inside = [(i, i ^ 1) for i in range(count)]
    first, second = chip_swaps(count)
    dma = pltpu.SemaphoreType.DMA
    edge_t = ((edges, width), BF)
    rim_t = ((half, width), BF)
    grad_t = ((atoms, width), BF)
    far_send, near_send, nbr, cnt = call(
        head_kernel,
        "head",
        (features, neighbours.T, counts.reshape(2, half)),
        [rim_t, rim_t, ((slots, atoms), jnp.int32), ((2, half), jnp.int32)],
        4,
        scratch=[dma((4,))],
        in_specs=[HB] * 3,
        flops=10**12,
    )
    far_first = lax.ppermute(far_send, "cell", first)
    far_second = lax.ppermute(far_send, "cell", second)
    near = lax.ppermute(near_send, "cell", inside)
    pick_t = ((edges, 4 * half), BF)
    edge_refs = (
        nbr, cnt, radial.reshape(atoms * slots, basis), cotangent.reshape(atoms * slots, entries),
        w_radial, w_block,
    )
    far_pick, total, gate, dgate, selfs, own = call(
        functools.partial(front_kernel, slots=slots),
        "front",
        edge_refs + (features, w_self, w_neighbour),
        [pick_t, edge_t, edge_t, edge_t, grad_t, grad_t],
        16,
    )
    side_t = [edge_t, edge_t, rim_t]
    near_msg, near_adj, near_rim, near_pick = call(
        functools.partial(near_kernel, slots=slots),
        "near",
        edge_refs + (near, w_neighbour, selfs, own),
        side_t + [pick_t],
        16,
        scratch=[pltpu.VMEM((edges, width), BF)] * 3,
    )
    near_back = lax.ppermute(near_rim, "cell", inside)
    far_msg, far_adj, far_rim = call(
        functools.partial(far_kernel, count=count),
        "far",
        (far_second, far_first, w_neighbour, selfs, total, gate, dgate, far_pick, near_msg),
        side_t,
        12,
    )
    far_back_second = lax.ppermute(far_rim, "cell", second)
    far_back_first = lax.ppermute(far_rim, "cell", first)
    blocks, grad = call(
        own_kernel,
        "own",
        (near_msg, far_msg, near_adj, far_adj, near_pick, far_pick, w_self, w_neighbour, w_block),
        [((2 * edges, entries), BF), ((atoms, width), F32)],
        16,
        scratch=[
            pltpu.VMEM((edges, entries), BF),
            pltpu.VMEM((edges, entries), BF),
            pltpu.VMEM((atoms, width), BF),
            dma((2,)),
        ],
        out_specs=[HB, VM],
    )
    (feat_grad,) = call(
        functools.partial(last_kernel, count=count),
        "last",
        (far_back_second, far_back_first, near_back, grad, w_neighbour),
        [grad_t],
        4,
        scratch=[pltpu.VMEM((atoms, width), BF), dma],
        out_specs=[HB],
    )
    return blocks.reshape(atoms, slots, entries), feat_grad


def solution(mesh):
    in_specs = (
        P("cell", None),
        P("cell", None, None),
        P("cell", None),
        P("cell"),
        P("cell", None, None),
        P(),
        P(),
        P(),
        P(),
    )
    out_specs = (P("cell", None, None), P("cell", None))
    return jax.shard_map(
        functools.partial(body, mesh.shape["cell"]),
        mesh=mesh, in_specs=in_specs, out_specs=out_specs, check_vma=False,
    )
```

```python
import functools

import jax
import jax.numpy as jnp
from jax import lax
from jax.experimental import pallas as pl
from jax.experimental.pallas import tpu as pltpu
from jax.sharding import PartitionSpec as P

BF = jnp.bfloat16
F32 = jnp.float32


def mm(a, b):
    return jnp.dot(a, b, preferred_element_type=F32)


def mm_nt(a, b):
    return lax.dot_general(a, b, (((1,), (1,)), ((), ())), preferred_element_type=F32)


def mm_tn(a, b):
    return lax.dot_general(a, b, (((0,), (0,)), ((), ())), preferred_element_type=F32)


def swaps(pairs):
    return [edge for a, b in pairs for edge in ((a, b), (b, a))]


def in_first(device):
    return ((device + 1) // 2 + 1) // 4 % 2 == 0


def chip_swaps(count):
    across = [(i, i + 1) for i in range(1, count - 1, 2)]
    if count < 16 or count % 8:
        return swaps(across), swaps(across)
    both = []
    for first in (True, False):
        pairs = [pair for pair in across if in_first(pair[0]) == first]
        busy = {device for pair in pairs for device in pair}
        rest = [device for device in range(count) if device not in busy]
        both.append(swaps(pairs + list(zip(rest[::2], rest[1::2]))))
    return both


def from_across(count, first_ref, second_ref):
    device = lax.axis_index("cell")
    value = jnp.where(in_first(device), first_ref[...], second_ref[...])
    inner = (device > 0) & (device < count - 1)
    return jnp.where(inner, value, jnp.zeros_like(value))


def halves(half):
    parity = lax.rem(lax.axis_index("cell"), 2)
    near, far = 1 - parity, parity
    return near, far, pl.multiple_of(near * half, half), pl.multiple_of(far * half, half)


def picker(nbr, count_row, base, half, slots):
    local = nbr - base
    own = (local >= 0) & (local < 2 * half)
    target = jnp.where(own, local, 2 * half + (local & (half - 1)))
    live = lax.broadcasted_iota(jnp.int32, (slots, half), 0) < count_row
    target = jnp.where(live, (target - half).astype(F32), -2.0 * half).astype(BF)
    edges = half * slots
    row = lax.broadcasted_iota(jnp.int32, (edges, half), 0)
    lane = lax.broadcasted_iota(jnp.int32, (edges, half), 1)
    one, zero = jnp.ones((), BF), jnp.zeros((), BF)
    lane_b = lane.astype(F32).astype(BF)
    same_atom = jnp.where(lane_b == (row // slots).astype(F32).astype(BF), one, zero)
    spread = mm_nt(same_atom, target)
    slot_lane = lax.broadcasted_iota(jnp.int32, (edges, slots), 1)
    slot_row = lax.broadcasted_iota(jnp.int32, (edges, slots), 0)
    mine = jnp.where((slot_row & (slots - 1)) == slot_lane, spread, 0.0)
    target = jnp.sum(mine, axis=1, keepdims=True)
    target = jnp.broadcast_to(target, (edges, half)).astype(BF)
    low, high, halo = [
        jnp.where(target == lane_b + BF(half * (j - 1)), one, zero) for j in range(3)
    ]
    mine = jnp.where(target > BF(-1.5 * half), same_atom, zero)
    return jnp.concatenate([low, high, mine, halo], axis=1)


def activation(total, half_gate, half_dgate):
    h = total * half_gate
    t = jnp.tanh(h)
    ht = h * t
    return h + ht, half_dgate * (t + BF(1.0)) * (h - ht + BF(1.0))


def head_kernel(feat_hbm, nbr_hbm, cnt_hbm, far_ref, near_ref, nbr_ref, cnt_ref, sems):
    half = far_ref.shape[0]
    _, _, near_off, far_off = halves(half)
    pairs = [
        (feat_hbm.at[pl.ds(far_off, half)], far_ref),
        (feat_hbm.at[pl.ds(near_off, half)], near_ref),
        (nbr_hbm, nbr_ref),
        (cnt_hbm, cnt_ref),
    ]
    copies = [pltpu.make_async_copy(src, dst, sems.at[n]) for n, (src, dst) in enumerate(pairs)]
    for copy in copies:
        copy.start()
    for copy in copies:
        copy.wait()


def prepare(half_index, own, refs, outs, slots):
    nbr_ref, cnt_ref, rad_ref, cot_ref, wrad_ref, wblk_ref = refs
    pick_ref, sum_ref, gate_ref, dgate_ref = outs
    edges = pick_ref.shape[0]
    half = edges // slots
    off = pl.multiple_of(half_index * half, half)
    rows = pl.ds(pl.multiple_of(half_index * edges, edges), edges)
    pick_ref[...] = picker(
        nbr_ref[:, pl.ds(off, half)],
        cnt_ref[pl.ds(half_index, 1), :],
        lax.axis_index("cell") * (2 * half),
        half,
        slots,
    )
    gate = mm(rad_ref[rows, :], wrad_ref[...] * BF(0.5))
    gate_ref[...] = gate.astype(BF)
    sum_ref[...] = mm(pick_ref[:, : 2 * half], own).astype(BF)
    dgate_ref[...] = (mm_nt(cot_ref[rows, :], wblk_ref[...]) * gate).astype(BF)


def front_kernel(
    nbr_ref, cnt_ref, rad_ref, cot_ref, wrad_ref, wblk_ref, feat_ref, wself_ref, wnbr_ref,
    pick_ref, sum_ref, gate_ref, dgate_ref, self_ref, own_ref,
    *, slots,
):
    _, far, _, _ = halves(feat_ref.shape[0] // 2)
    own = mm(feat_ref[...], wnbr_ref[...]).astype(BF)
    own_ref[...] = own
    self_ref[...] = mm(feat_ref[...], wself_ref[...]).astype(BF)
    refs = (nbr_ref, cnt_ref, rad_ref, cot_ref, wrad_ref, wblk_ref)
    prepare(far, own, refs, (pick_ref, sum_ref, gate_ref, dgate_ref), slots)


def side(halo, half_index, refs, msg_ref, adj_ref, rim_ref):
    self_ref, sum_ref, gate_ref, dgate_ref, pick_ref = refs
    half = rim_ref.shape[0]
    edges = msg_ref.shape[0]
    table = jnp.concatenate(
        [self_ref[pl.ds(pl.multiple_of(half_index * half, half), half), :], halo], axis=0
    )
    step = edges // 2
    chunks = [slice(n * step, (n + 1) * step) for n in range(2)]
    parts = [mm(pick_ref[rows, 2 * half :], table).astype(BF) for rows in chunks]
    for rows, part in zip(chunks, parts):
        message, adj = activation(sum_ref[rows, :] + part, gate_ref[rows, :], dgate_ref[rows, :])
        msg_ref[rows, :] = message
        adj_ref[rows, :] = adj
    rim_ref[...] = mm_tn(pick_ref[:, 3 * half :], adj_ref[...]).astype(BF)


def near_kernel(
    nbr_ref, cnt_ref, rad_ref, cot_ref, wrad_ref, wblk_ref, near_ref, wnbr_ref, self_ref, own_ref,
    msg_ref, adj_ref, rim_ref, pick_ref,
    sum_ref, gate_ref, dgate_ref,
    *, slots,
):
    near, _, _, _ = halves(rim_ref.shape[0])
    refs = (nbr_ref, cnt_ref, rad_ref, cot_ref, wrad_ref, wblk_ref)
    prepare(near, own_ref[...], refs, (pick_ref, sum_ref, gate_ref, dgate_ref), slots)
    halo = mm(near_ref[...], wnbr_ref[...]).astype(BF)
    side(halo, near, (self_ref, sum_ref, gate_ref, dgate_ref, pick_ref), msg_ref, adj_ref, rim_ref)


def far_kernel(
    second_ref, first_ref, wnbr_ref, self_ref, sum_ref, gate_ref, dgate_ref, pick_ref, order_ref,
    msg_ref, adj_ref, rim_ref,
    *, count,
):
    _, far, _, _ = halves(rim_ref.shape[0])
    halo = mm(from_across(count, first_ref, second_ref), wnbr_ref[...]).astype(BF)
    side(halo, far, (self_ref, sum_ref, gate_ref, dgate_ref, pick_ref), msg_ref, adj_ref, rim_ref)


def own_kernel(
    nearmsg_ref, farmsg_ref, nearadj_ref, faradj_ref, nearpick_ref, farpick_ref, wself_ref, wnbr_ref, wblk_ref,
    blocks_hbm, grad_ref, turned_ref,
    nearblk_ref, farblk_ref, selfsum_ref, sems,
):
    edges = farmsg_ref.shape[0]
    atoms = grad_ref.shape[0]
    half = atoms // 2
    near, far, near_off, far_off = halves(half)
    near_edge = pl.multiple_of(near * edges, edges)
    far_edge = pl.multiple_of(far * edges, edges)
    farblk_ref[...] = mm(farmsg_ref[...], wblk_ref[...]).astype(BF)
    far_copy = pltpu.make_async_copy(farblk_ref, blocks_hbm.at[pl.ds(far_edge, edges)], sems.at[0])
    far_copy.start()
    nearblk_ref[...] = mm(nearmsg_ref[...], wblk_ref[...]).astype(BF)
    near_copy = pltpu.make_async_copy(
        nearblk_ref, blocks_hbm.at[pl.ds(near_edge, edges)], sems.at[1]
    )
    near_copy.start()

    @pl.when(lax.axis_index("cell") >= 0)
    def _():
        near_back = mm_tn(nearpick_ref[:, : atoms + half], nearadj_ref[...])
        far_back = mm_tn(farpick_ref[:, : atoms + half], faradj_ref[...])
        selfsum_ref[pl.ds(near_off, half), :] = near_back[atoms:].astype(BF)
        selfsum_ref[pl.ds(far_off, half), :] = far_back[atoms:].astype(BF)
        total = (near_back[:atoms] + far_back[:atoms]).astype(BF)
        grad_ref[...] = mm_nt(total, wnbr_ref[...]) + mm_nt(selfsum_ref[...], wself_ref[...])
        turned_ref[...] = wnbr_ref[...].T

    near_copy.wait()
    far_copy.wait()


def last_kernel(second_ref, first_ref, near_ref, grad_ref, turned_ref, out_hbm, out_ref, sem, *, count):
    half = near_ref.shape[0]
    _, _, near_off, far_off = halves(half)
    rims = jnp.concatenate([from_across(count, first_ref, second_ref), near_ref[...]], axis=0)
    grads = jnp.concatenate(
        [grad_ref[pl.ds(far_off, half), :], grad_ref[pl.ds(near_off, half), :]], axis=0
    )
    total = (grads + mm(rims, turned_ref[...])).astype(BF)
    out_ref[pl.ds(far_off, half), :] = total[:half]
    out_ref[pl.ds(near_off, half), :] = total[half:]
    copy = pltpu.make_async_copy(out_ref, out_hbm, sem)
    copy.start()
    copy.wait()


VM = pl.BlockSpec(memory_space=pltpu.VMEM)
HB = pl.BlockSpec(memory_space=pltpu.HBM)


def call(kernel, name, inputs, outs, megabytes, scratch=(), in_specs=None, out_specs=None, flops=0):
    in_specs = in_specs or [VM] * len(inputs)
    inputs = [
        pltpu.with_memory_space_constraint(x, pltpu.HBM) if spec is HB else x
        for x, spec in zip(inputs, in_specs)
    ]
    return pl.pallas_call(
        kernel,
        name=name,
        out_shape=[jax.ShapeDtypeStruct(shape, dtype) for shape, dtype in outs],
        in_specs=in_specs,
        out_specs=out_specs or [VM] * len(outs),
        scratch_shapes=list(scratch),
        cost_estimate=pl.CostEstimate(flops=flops, bytes_accessed=0, transcendentals=0),
        compiler_params=pltpu.CompilerParams(vmem_limit_bytes=megabytes * 1024 * 1024),
    )(*inputs)


def body(count, features, radial, neighbours, counts, cotangent, w_self, w_neighbour, w_radial, w_block):
    atoms, width = features.shape
    slots = neighbours.shape[1]
    half = atoms // 2
    edges = half * slots
    entries = w_block.shape[1]
    basis = radial.shape[2]
    inside = [(i, i ^ 1) for i in range(count)]
    first, second = chip_swaps(count)
    dma = pltpu.SemaphoreType.DMA
    edge_t = ((edges, width), BF)
    rim_t = ((half, width), BF)
    grad_t = ((atoms, width), BF)
    far_send, near_send, nbr, cnt = call(
        head_kernel,
        "head",
        (features, neighbours.T, counts.reshape(2, half)),
        [rim_t, rim_t, ((slots, atoms), jnp.int32), ((2, half), jnp.int32)],
        4,
        scratch=[dma((4,))],
        in_specs=[HB] * 3,
        flops=10**12,
    )
    far_first = lax.ppermute(far_send, "cell", first)
    far_second = lax.ppermute(far_send, "cell", second)
    near = lax.ppermute(near_send, "cell", inside)
    pick_t = ((edges, 4 * half), BF)
    edge_refs = (
        nbr, cnt, radial.reshape(atoms * slots, basis), cotangent.reshape(atoms * slots, entries),
        w_radial, w_block,
    )
    far_pick, total, gate, dgate, selfs, own = call(
        functools.partial(front_kernel, slots=slots),
        "front",
        edge_refs + (features, w_self, w_neighbour),
        [pick_t, edge_t, edge_t, edge_t, grad_t, grad_t],
        16,
    )
    side_t = [edge_t, edge_t, rim_t]
    near_msg, near_adj, near_rim, near_pick = call(
        functools.partial(near_kernel, slots=slots),
        "near",
        edge_refs + (near, w_neighbour, selfs, own),
        side_t + [pick_t],
        16,
        scratch=[pltpu.VMEM((edges, width), BF)] * 3,
    )
    near_back = lax.ppermute(near_rim, "cell", inside)
    far_msg, far_adj, far_rim = call(
        functools.partial(far_kernel, count=count),
        "far",
        (far_second, far_first, w_neighbour, selfs, total, gate, dgate, far_pick, near_msg),
        side_t,
        12,
    )
    far_back_second = lax.ppermute(far_rim, "cell", second)
    far_back_first = lax.ppermute(far_rim, "cell", first)
    blocks, grad, turned = call(
        own_kernel,
        "own",
        (near_msg, far_msg, near_adj, far_adj, near_pick, far_pick, w_self, w_neighbour, w_block),
        [((2 * edges, entries), BF), ((atoms, width), F32), ((width, width), BF)],
        16,
        scratch=[
            pltpu.VMEM((edges, entries), BF),
            pltpu.VMEM((edges, entries), BF),
            pltpu.VMEM((atoms, width), BF),
            dma((2,)),
        ],
        out_specs=[HB, VM, VM],
    )
    (feat_grad,) = call(
        functools.partial(last_kernel, count=count),
        "last",
        (far_back_second, far_back_first, near_back, grad, turned),
        [grad_t],
        4,
        scratch=[pltpu.VMEM((atoms, width), BF), dma],
        out_specs=[HB],
    )
    return blocks.reshape(atoms, slots, entries), feat_grad


def solution(mesh):
    in_specs = (
        P("cell", None),
        P("cell", None, None),
        P("cell", None),
        P("cell"),
        P("cell", None, None),
        P(),
        P(),
        P(),
        P(),
    )
    out_specs = (P("cell", None, None), P("cell", None))
    return jax.shard_map(
        functools.partial(body, mesh.shape["cell"]),
        mesh=mesh, in_specs=in_specs, out_specs=out_specs, check_vma=False,
    )
```

```python
import functools

import jax
import jax.numpy as jnp
from jax import lax
from jax.experimental import pallas as pl
from jax.experimental.pallas import tpu as pltpu
from jax.sharding import PartitionSpec as P

BF = jnp.bfloat16
F32 = jnp.float32


def mm(a, b):
    return jnp.dot(a, b, preferred_element_type=F32)


def mm_nt(a, b):
    return lax.dot_general(a, b, (((1,), (1,)), ((), ())), preferred_element_type=F32)


def mm_tn(a, b):
    return lax.dot_general(a, b, (((0,), (0,)), ((), ())), preferred_element_type=F32)


def swaps(pairs):
    return [edge for a, b in pairs for edge in ((a, b), (b, a))]


def in_first(device):
    return ((device + 1) // 2 + 1) // 4 % 2 == 0


def chip_swaps(count):
    across = [(i, i + 1) for i in range(1, count - 1, 2)]
    if count < 16 or count % 8:
        return swaps(across), swaps(across)
    both = []
    for first in (True, False):
        pairs = [pair for pair in across if in_first(pair[0]) == first]
        busy = {device for pair in pairs for device in pair}
        rest = [device for device in range(count) if device not in busy]
        both.append(swaps(pairs + list(zip(rest[::2], rest[1::2]))))
    return both


def from_across(count, first_ref, second_ref):
    device = lax.axis_index("cell")
    value = jnp.where(in_first(device), first_ref[...], second_ref[...])
    inner = (device > 0) & (device < count - 1)
    return jnp.where(inner, value, jnp.zeros_like(value))


def halves(half):
    parity = lax.rem(lax.axis_index("cell"), 2)
    near, far = 1 - parity, parity
    return near, far, pl.multiple_of(near * half, half), pl.multiple_of(far * half, half)


def picker(nbr, count_row, base, half, slots):
    local = nbr - base
    own = (local >= 0) & (local < 2 * half)
    target = jnp.where(own, local, 2 * half + (local & (half - 1)))
    live = lax.broadcasted_iota(jnp.int32, (slots, half), 0) < count_row
    target = jnp.where(live, (target - half).astype(F32), -2.0 * half).astype(BF)
    edges = half * slots
    row = lax.broadcasted_iota(jnp.int32, (edges, half), 0)
    lane = lax.broadcasted_iota(jnp.int32, (edges, half), 1)
    one, zero = jnp.ones((), BF), jnp.zeros((), BF)
    lane_b = lane.astype(F32).astype(BF)
    same_atom = jnp.where(lane_b == (row // slots).astype(F32).astype(BF), one, zero)
    spread = mm_nt(same_atom, target)
    slot_lane = lax.broadcasted_iota(jnp.int32, (edges, slots), 1)
    slot_row = lax.broadcasted_iota(jnp.int32, (edges, slots), 0)
    mine = jnp.where((slot_row & (slots - 1)) == slot_lane, spread, 0.0)
    target = jnp.sum(mine, axis=1, keepdims=True)
    target = jnp.broadcast_to(target, (edges, half)).astype(BF)
    low, high, halo = [
        jnp.where(target == lane_b + BF(half * (j - 1)), one, zero) for j in range(3)
    ]
    mine = jnp.where(target > BF(-1.5 * half), same_atom, zero)
    return jnp.concatenate([low, high, mine, halo], axis=1)


def activation(total, half_gate, half_dgate):
    h = total * half_gate
    t = jnp.tanh(h)
    ht = h * t
    return h + ht, half_dgate * (t + BF(1.0)) * (h - ht + BF(1.0))


def head_kernel(feat_hbm, nbr_hbm, cnt_hbm, far_ref, near_ref, nbr_ref, cnt_ref, sems):
    half = far_ref.shape[0]
    _, _, near_off, far_off = halves(half)
    pairs = [
        (feat_hbm.at[pl.ds(far_off, half)], far_ref),
        (feat_hbm.at[pl.ds(near_off, half)], near_ref),
        (nbr_hbm, nbr_ref),
        (cnt_hbm, cnt_ref),
    ]
    copies = [pltpu.make_async_copy(src, dst, sems.at[n]) for n, (src, dst) in enumerate(pairs)]
    for copy in copies:
        copy.start(priority=1)
    for copy in copies:
        copy.wait()


def prepare(half_index, own, refs, outs, slots):
    nbr_ref, cnt_ref, rad_ref, cot_ref, wrad_ref, wblk_ref = refs
    pick_ref, sum_ref, gate_ref, dgate_ref = outs
    edges = pick_ref.shape[0]
    half = edges // slots
    off = pl.multiple_of(half_index * half, half)
    rows = pl.ds(pl.multiple_of(half_index * edges, edges), edges)
    pick_ref[...] = picker(
        nbr_ref[:, pl.ds(off, half)],
        cnt_ref[pl.ds(half_index, 1), :],
        lax.axis_index("cell") * (2 * half),
        half,
        slots,
    )
    gate = mm(rad_ref[rows, :], wrad_ref[...] * BF(0.5))
    gate_ref[...] = gate.astype(BF)
    sum_ref[...] = mm(pick_ref[:, : 2 * half], own).astype(BF)
    dgate_ref[...] = (mm_nt(cot_ref[rows, :], wblk_ref[...]) * gate).astype(BF)


def front_kernel(
    nbr_ref, cnt_ref, rad_ref, cot_ref, wrad_ref, wblk_ref, feat_ref, wself_ref, wnbr_ref,
    pick_ref, sum_ref, gate_ref, dgate_ref, self_ref, own_ref,
    *, slots,
):
    _, far, _, _ = halves(feat_ref.shape[0] // 2)
    own = mm(feat_ref[...], wnbr_ref[...]).astype(BF)
    own_ref[...] = own
    self_ref[...] = mm(feat_ref[...], wself_ref[...]).astype(BF)
    refs = (nbr_ref, cnt_ref, rad_ref, cot_ref, wrad_ref, wblk_ref)
    prepare(far, own, refs, (pick_ref, sum_ref, gate_ref, dgate_ref), slots)


def side(halo, half_index, refs, msg_ref, adj_ref, rim_ref):
    self_ref, sum_ref, gate_ref, dgate_ref, pick_ref = refs
    half = rim_ref.shape[0]
    edges = msg_ref.shape[0]
    table = jnp.concatenate(
        [self_ref[pl.ds(pl.multiple_of(half_index * half, half), half), :], halo], axis=0
    )
    step = edges // 2
    chunks = [slice(n * step, (n + 1) * step) for n in range(2)]
    parts = [mm(pick_ref[rows, 2 * half :], table).astype(BF) for rows in chunks]
    for rows, part in zip(chunks, parts):
        message, adj = activation(sum_ref[rows, :] + part, gate_ref[rows, :], dgate_ref[rows, :])
        msg_ref[rows, :] = message
        adj_ref[rows, :] = adj
    rim_ref[...] = mm_tn(pick_ref[:, 3 * half :], adj_ref[...]).astype(BF)


def near_kernel(
    nbr_ref, cnt_ref, rad_ref, cot_ref, wrad_ref, wblk_ref, near_ref, wnbr_ref, self_ref, own_ref,
    msg_ref, adj_ref, rim_ref, pick_ref,
    sum_ref, gate_ref, dgate_ref,
    *, slots,
):
    near, _, _, _ = halves(rim_ref.shape[0])
    refs = (nbr_ref, cnt_ref, rad_ref, cot_ref, wrad_ref, wblk_ref)
    prepare(near, own_ref[...], refs, (pick_ref, sum_ref, gate_ref, dgate_ref), slots)
    halo = mm(near_ref[...], wnbr_ref[...]).astype(BF)
    side(halo, near, (self_ref, sum_ref, gate_ref, dgate_ref, pick_ref), msg_ref, adj_ref, rim_ref)


def far_kernel(
    second_ref, first_ref, wnbr_ref, self_ref, sum_ref, gate_ref, dgate_ref, pick_ref, order_ref,
    msg_ref, adj_ref, rim_ref,
    *, count,
):
    _, far, _, _ = halves(rim_ref.shape[0])
    halo = mm(from_across(count, first_ref, second_ref), wnbr_ref[...]).astype(BF)
    side(halo, far, (self_ref, sum_ref, gate_ref, dgate_ref, pick_ref), msg_ref, adj_ref, rim_ref)


def own_kernel(
    nearmsg_ref, farmsg_ref, nearadj_ref, faradj_ref, nearpick_ref, farpick_ref, wself_ref, wnbr_ref, wblk_ref,
    blocks_hbm, grad_ref, turned_ref,
    nearblk_ref, farblk_ref, selfsum_ref, sems,
):
    edges = farmsg_ref.shape[0]
    atoms = grad_ref.shape[0]
    half = atoms // 2
    near, far, near_off, far_off = halves(half)
    near_edge = pl.multiple_of(near * edges, edges)
    far_edge = pl.multiple_of(far * edges, edges)
    farblk_ref[...] = mm(farmsg_ref[...], wblk_ref[...]).astype(BF)
    far_copy = pltpu.make_async_copy(farblk_ref, blocks_hbm.at[pl.ds(far_edge, edges)], sems.at[0])
    far_copy.start()
    nearblk_ref[...] = mm(nearmsg_ref[...], wblk_ref[...]).astype(BF)
    near_copy = pltpu.make_async_copy(
        nearblk_ref, blocks_hbm.at[pl.ds(near_edge, edges)], sems.at[1]
    )
    near_copy.start()

    @pl.when(lax.axis_index("cell") >= 0)
    def _():
        near_back = mm_tn(nearpick_ref[:, : atoms + half], nearadj_ref[...])
        far_back = mm_tn(farpick_ref[:, : atoms + half], faradj_ref[...])
        selfsum_ref[pl.ds(near_off, half), :] = near_back[atoms:].astype(BF)
        selfsum_ref[pl.ds(far_off, half), :] = far_back[atoms:].astype(BF)
        total = (near_back[:atoms] + far_back[:atoms]).astype(BF)
        grad_ref[...] = mm_nt(total, wnbr_ref[...]) + mm_nt(selfsum_ref[...], wself_ref[...])
        turned_ref[...] = wnbr_ref[...].T

    near_copy.wait()
    far_copy.wait()


def last_kernel(second_ref, first_ref, near_ref, grad_ref, turned_ref, out_hbm, out_ref, sem, *, count):
    half = near_ref.shape[0]
    _, _, near_off, far_off = halves(half)
    rims = jnp.concatenate([from_across(count, first_ref, second_ref), near_ref[...]], axis=0)
    grads = jnp.concatenate(
        [grad_ref[pl.ds(far_off, half), :], grad_ref[pl.ds(near_off, half), :]], axis=0
    )
    total = (grads + mm(rims, turned_ref[...])).astype(BF)
    out_ref[pl.ds(far_off, half), :] = total[:half]
    out_ref[pl.ds(near_off, half), :] = total[half:]
    copy = pltpu.make_async_copy(out_ref, out_hbm, sem)
    copy.start()
    copy.wait()


VM = pl.BlockSpec(memory_space=pltpu.VMEM)
HB = pl.BlockSpec(memory_space=pltpu.HBM)


def call(kernel, name, inputs, outs, megabytes, scratch=(), in_specs=None, out_specs=None, flops=0):
    in_specs = in_specs or [VM] * len(inputs)
    inputs = [
        pltpu.with_memory_space_constraint(x, pltpu.HBM) if spec is HB else x
        for x, spec in zip(inputs, in_specs)
    ]
    return pl.pallas_call(
        kernel,
        name=name,
        out_shape=[jax.ShapeDtypeStruct(shape, dtype) for shape, dtype in outs],
        in_specs=in_specs,
        out_specs=out_specs or [VM] * len(outs),
        scratch_shapes=list(scratch),
        cost_estimate=pl.CostEstimate(flops=flops, bytes_accessed=0, transcendentals=0),
        compiler_params=pltpu.CompilerParams(vmem_limit_bytes=megabytes * 1024 * 1024),
    )(*inputs)


def body(count, features, radial, neighbours, counts, cotangent, w_self, w_neighbour, w_radial, w_block):
    atoms, width = features.shape
    slots = neighbours.shape[1]
    half = atoms // 2
    edges = half * slots
    entries = w_block.shape[1]
    basis = radial.shape[2]
    inside = [(i, i ^ 1) for i in range(count)]
    first, second = chip_swaps(count)
    dma = pltpu.SemaphoreType.DMA
    edge_t = ((edges, width), BF)
    rim_t = ((half, width), BF)
    grad_t = ((atoms, width), BF)
    far_send, near_send, nbr, cnt = call(
        head_kernel,
        "head",
        (features, neighbours.T, counts.reshape(2, half)),
        [rim_t, rim_t, ((slots, atoms), jnp.int32), ((2, half), jnp.int32)],
        4,
        scratch=[dma((4,))],
        in_specs=[HB] * 3,
        flops=10**12,
    )
    far_first = lax.ppermute(far_send, "cell", first)
    far_second = lax.ppermute(far_send, "cell", second)
    near = lax.ppermute(near_send, "cell", inside)
    pick_t = ((edges, 4 * half), BF)
    edge_refs = (
        nbr, cnt, radial.reshape(atoms * slots, basis), cotangent.reshape(atoms * slots, entries),
        w_radial, w_block,
    )
    far_pick, total, gate, dgate, selfs, own = call(
        functools.partial(front_kernel, slots=slots),
        "front",
        edge_refs + (features, w_self, w_neighbour),
        [pick_t, edge_t, edge_t, edge_t, grad_t, grad_t],
        16,
    )
    side_t = [edge_t, edge_t, rim_t]
    near_msg, near_adj, near_rim, near_pick = call(
        functools.partial(near_kernel, slots=slots),
        "near",
        edge_refs + (near, w_neighbour, selfs, own),
        side_t + [pick_t],
        16,
        scratch=[pltpu.VMEM((edges, width), BF)] * 3,
    )
    near_back = lax.ppermute(near_rim, "cell", inside)
    far_msg, far_adj, far_rim = call(
        functools.partial(far_kernel, count=count),
        "far",
        (far_second, far_first, w_neighbour, selfs, total, gate, dgate, far_pick, near_msg),
        side_t,
        12,
    )
    far_back_second = lax.ppermute(far_rim, "cell", second)
    far_back_first = lax.ppermute(far_rim, "cell", first)
    blocks, grad, turned = call(
        own_kernel,
        "own",
        (near_msg, far_msg, near_adj, far_adj, near_pick, far_pick, w_self, w_neighbour, w_block),
        [((2 * edges, entries), BF), ((atoms, width), F32), ((width, width), BF)],
        16,
        scratch=[
            pltpu.VMEM((edges, entries), BF),
            pltpu.VMEM((edges, entries), BF),
            pltpu.VMEM((atoms, width), BF),
            dma((2,)),
        ],
        out_specs=[HB, VM, VM],
    )
    (feat_grad,) = call(
        functools.partial(last_kernel, count=count),
        "last",
        (far_back_second, far_back_first, near_back, grad, turned),
        [grad_t],
        4,
        scratch=[pltpu.VMEM((atoms, width), BF), dma],
        out_specs=[HB],
    )
    return blocks.reshape(atoms, slots, entries), feat_grad


def solution(mesh):
    in_specs = (
        P("cell", None),
        P("cell", None, None),
        P("cell", None),
        P("cell"),
        P("cell", None, None),
        P(),
        P(),
        P(),
        P(),
    )
    out_specs = (P("cell", None, None), P("cell", None))
    return jax.shard_map(
        functools.partial(body, mesh.shape["cell"]),
        mesh=mesh, in_specs=in_specs, out_specs=out_specs, check_vma=False,
    )
```
